256 devices in a mesh: dp: 8 (over y, x_hi), seq: 32 (over x_lo, z, core).
Axes of the slice: x: 4 (x_hi: 2, x_lo: 2; x = x_hi * 2 + x_lo), y: 4, z: 8, core: 2. Of those that a mesh axis runs over, the one named last changes fastest.
Arguments:
- query_lin: bfloat16 [32768, 4096], P(('dp', 'seq')), parts along dimension 0, may hold values from -6 to 6
- key_lin: bfloat16 [32768, 4096], P(('dp', 'seq')), parts along dimension 0, may hold values from -6 to 6
- value_lin: bfloat16 [32768, 4096], P(('dp', 'seq')), parts along dimension 0, may hold values from -100 to 100
- log_decay: bfloat16 [32768, 32], P(('dp', 'seq')), parts along dimension 0, may hold values from -2.2 to 0
- out_gate: bfloat16 [32768, 4096], P(('dp', 'seq')), parts along dimension 0, may hold values from -8 to 8
- norm_gain: float32 [4096], replicated, may hold values from 0.5 to 1.5
- state_in: float32 [256, 128, 128], P(('dp', 'seq')), parts along dimension 0, may hold values from -10 to 10
- query_soft: bfloat16 [32768, 4096], P(('dp', 'seq')), parts along dimension 0, may hold values from -4.5 to 4.5
- key_soft: bfloat16 [32768, 1024], P(('dp', 'seq')), parts along dimension 0, may hold values from -4.5 to 4.5
- value_soft: bfloat16 [32768, 1024], P(('dp', 'seq')), parts along dimension 0, may hold values from -6 to 6
Outputs:
- light_out: bfloat16 [32768, 4096], P(('dp', 'seq')), parts along dimension 0
- state_out: float32 [256, 128, 128], P(('dp', 'seq')), parts along dimension 0
- attn_out: bfloat16 [32768, 4096], P(('dp', 'seq')), parts along dimension 0
The draws below stay inside these ranges and needn't reach their ends.
There are 8 independent parts, one for each index of `dp`. The reference program is written for one: setup_inputs(seed, part) draws one part's arguments, and reference() takes and returns one part's arrays. A program takes and returns all parts, laid end to end along the dimension named above; an argument that names none is the same for every part. Nothing has to cross between parts.
All inputs are finite; a program needn't handle non-finite values.
Results may differ from the reference program's by a relative error of at most 0.009.
Values may be sent and summed in bfloat16 or wider, within the bound.
A program may use at most 192 MiB of HBM per device.

```python
import math
import jax
import jax.numpy as jnp
from jax import lax

HEADS = 32
KV_HEADS = 8
DH = 128
LHEADS = 32
BLK = 128
TOK_DEV = 128
WINDOW_TOKENS = 4096


def draw_query_soft(key, part):
    key = jax.random.fold_in(key, 41)
    table_entries = jnp.clip(jax.random.normal(key, (WINDOW_TOKENS, HEADS, DH), jnp.float32), -4.5, 4.5)
    return table_entries.reshape(WINDOW_TOKENS, HEADS * DH).astype(jnp.bfloat16)


def draw_key_soft(key, part):
    key = jax.random.fold_in(key, 43)
    table_entries = jnp.clip(jax.random.normal(key, (WINDOW_TOKENS, KV_HEADS, DH), jnp.float32), -4.5, 4.5)
    return table_entries.reshape(WINDOW_TOKENS, KV_HEADS * DH).astype(jnp.bfloat16)


def draw_value_lin(key, part):
    key = jax.random.fold_in(key, 47)
    width_all = LHEADS * DH
    table_entries = jnp.clip(jax.random.normal(key, (WINDOW_TOKENS, width_all), jnp.float32), -6.0, 6.0)
    return table_entries.astype(jnp.bfloat16)


def draw_log_decay(key, part):
    key = jax.random.fold_in(key, 53)
    fast_share = 0.5
    random_offset = jnp.exp(jax.random.uniform(jax.random.fold_in(key, 1), (WINDOW_TOKENS, LHEADS), jnp.float32, math.log(0.5), math.log(2.0)))
    fast = jax.random.uniform(jax.random.fold_in(key, 2), (LHEADS,), jnp.float32) < fast_share
    decay_rates = jnp.where(fast, 1.0 / 40.0, 0.5 / WINDOW_TOKENS)
    block_multiplier = jnp.exp(jax.random.uniform(jax.random.fold_in(key, 3), (WINDOW_TOKENS // TOK_DEV, LHEADS), jnp.float32, math.log(0.5), math.log(2.0)))
    block_multiplier = jnp.repeat(block_multiplier, TOK_DEV, axis=0)
    cluster_rows = jax.random.randint(jax.random.fold_in(key, 4), (3,), 0, WINDOW_TOKENS)
    cluster_depth = jax.random.uniform(jax.random.fold_in(key, 5), (3,), jnp.float32, math.log(0.5), math.log(0.8))
    token_positions = jnp.arange(WINDOW_TOKENS)[:, None]
    clusters = jnp.sum(jnp.where(token_positions == cluster_rows[None, :], cluster_depth[None, :], 0.0), axis=1, keepdims=True)
    table_entries = -decay_rates[None, :] * block_multiplier * random_offset + clusters
    return table_entries.astype(jnp.bfloat16)


def steps_of(rng, extent, cuts, smallest, high):
    factor_of = 1.0
    for position, parts in cuts:
        steps = jax.random.uniform(jax.random.fold_in(jax.random.fold_in(rng, 6), position), (parts,), jnp.float32, smallest / len(cuts), high / len(cuts))
        factor_of = factor_of * jnp.repeat(jnp.exp(steps), extent[position] // parts).reshape((-1,) + (1,) * (len(extent) - 1 - position))
    return factor_of


def centred(key, extent, width, limit, shards=(), dtype=jnp.bfloat16):
    entries = width * jax.random.normal(key, extent, jnp.float32)
    if shards:
        entries = entries * steps_of(key, extent, shards, -0.22, 0.18)
    return jnp.clip(entries, -limit, limit).astype(dtype)


def setup_inputs(seed: int = 0, part: int = 0) -> dict:
    arg_keys = jax.random.split(jax.random.key(seed), 11)
    part_keys = jax.random.split(jax.random.fold_in(arg_keys[10], part), 11)
    query_lin = centred(part_keys[0], (WINDOW_TOKENS, LHEADS * DH), 1.0, 6.0, ((0, 32),))
    key_lin = centred(part_keys[1], (WINDOW_TOKENS, LHEADS * DH), 1.0, 6.0, ((0, 32),))
    value_lin = draw_value_lin(jax.random.fold_in(jax.random.fold_in(arg_keys[10], part), 71), part)
    log_decay = draw_log_decay(jax.random.fold_in(jax.random.fold_in(arg_keys[10], part), 71), part)
    out_gate = centred(part_keys[4], (WINDOW_TOKENS, LHEADS * DH), 2.0, 8.0, ((0, 32),))
    norm_gain = jnp.clip(1.0 + 0.1 * jax.random.normal(arg_keys[5], (LHEADS * DH,), jnp.float32), 0.5, 1.5)
    state_in = centred(part_keys[6], (LHEADS, DH, DH), 2.0, 10.0, ((0, 32),), jnp.float32)
    query_soft = draw_query_soft(jax.random.fold_in(jax.random.fold_in(arg_keys[10], part), 71), part)
    key_soft = draw_key_soft(jax.random.fold_in(jax.random.fold_in(arg_keys[10], part), 71), part)
    value_soft = centred(part_keys[9], (WINDOW_TOKENS, KV_HEADS * DH), 1.0, 6.0, ((0, 32),))
    return {"query_lin": query_lin, "key_lin": key_lin, "value_lin": value_lin, "log_decay": log_decay, "out_gate": out_gate, "norm_gain": norm_gain, "state_in": state_in, "query_soft": query_soft, "key_soft": key_soft, "value_soft": value_soft}


norm_eps = 1e-06

def lightning_blocks(queries, keys_act, values, decays, initial, block_len):
    row_count, head_count, head_width = queries.shape
    block_count = row_count // block_len
    shape_four = (block_count, block_len, head_count, head_width)
    query_blocks = queries.reshape(shape_four).astype(jnp.float32)
    key_blocks = keys_act.reshape(shape_four).astype(jnp.float32)
    value_blocks = values.reshape(shape_four).astype(jnp.float32)
    running = jnp.cumsum(decays.reshape(block_count, block_len, head_count), axis=1)
    closing = running[:, -1, :]
    scores = jnp.einsum('bthd,bshd->bhts', query_blocks, key_blocks, precision=lax.Precision.HIGHEST)
    ordered = jnp.transpose(running, (0, 2, 1))
    spread = ordered[:, :, :, None] - ordered[:, :, None, :]
    causal = jnp.arange(block_len)[:, None] >= jnp.arange(block_len)[None, :]
    damping = jnp.where(causal, jnp.exp(jnp.where(causal, spread, 0.0)), 0.0)
    damped = (scores * damping).astype(jnp.bfloat16).astype(jnp.float32)
    inner = jnp.einsum('bhts,bshd->bthd', damped, value_blocks, precision=lax.Precision.HIGHEST)
    key_decayed = (key_blocks * jnp.exp(closing[:, None, :] - running)[..., None]).astype(jnp.bfloat16).astype(jnp.float32)
    block_states = jnp.einsum('bshd,bshe->bhde', key_decayed, value_blocks, precision=lax.Precision.HIGHEST)
    query_decayed = query_blocks * jnp.exp(running)[..., None]
    block_decay = jnp.exp(closing)

    def advance(carried_state, block_items):
        query_part, state_part, decay_part = block_items
        reached = jnp.einsum('thd,hde->the', query_part, carried_state, precision=lax.Precision.HIGHEST)
        return (decay_part[:, None, None] * carried_state + state_part, reached)
    final_state, reached = lax.scan(advance, initial, (query_decayed, block_states, block_decay))
    return ((inner + reached).reshape(row_count, head_count, head_width), final_state)

def finish_rows(mixed_rows, out_gate, norm_gain):
    mean_square = lax.optimization_barrier(jnp.mean(mixed_rows * mixed_rows, axis=1, keepdims=True))
    normed = mixed_rows * lax.rsqrt(mean_square + norm_eps)
    gated = normed * norm_gain.astype(jnp.float32) * jax.nn.sigmoid(out_gate.astype(jnp.float32))
    return gated.astype(jnp.bfloat16)

def masked_softmax(scores, causal):
    masked = jnp.where(causal, scores, -jnp.inf)
    row_max = lax.optimization_barrier(jnp.max(masked, axis=-1, keepdims=True))
    raised = jnp.exp(masked - row_max)
    row_total = lax.optimization_barrier(jnp.sum(raised, axis=-1, keepdims=True))
    return (raised.astype(jnp.bfloat16), row_total)

def soft_attention(query_soft, key_soft, value_soft):
    group_size = HEADS // KV_HEADS
    query_heads = jnp.transpose(query_soft.reshape(WINDOW_TOKENS, HEADS, DH), (1, 0, 2))
    key_heads = jnp.repeat(jnp.transpose(key_soft.reshape(WINDOW_TOKENS, KV_HEADS, DH), (1, 0, 2)), group_size, axis=0)
    value_heads = jnp.repeat(jnp.transpose(value_soft.reshape(WINDOW_TOKENS, KV_HEADS, DH), (1, 0, 2)), group_size, axis=0)
    block_rows = math.gcd(WINDOW_TOKENS, 512)
    score_scale = DH ** (-0.5)

    def one_head(operands):
        query_one, key_one, value_one = operands
        pieces = []
        for offset in range(0, WINDOW_TOKENS, block_rows):
            stop_row = offset + block_rows
            scores = jnp.dot(query_one[offset:stop_row], key_one[:stop_row].T, preferred_element_type=jnp.float32) * score_scale
            causal = (offset + jnp.arange(block_rows))[:, None] >= jnp.arange(stop_row)[None, :]
            raised, row_total = masked_softmax(scores, causal)
            summed = jnp.dot(raised, value_one[:stop_row], preferred_element_type=jnp.float32)
            pieces.append((summed / row_total).astype(jnp.bfloat16))
        return jnp.concatenate(pieces, axis=0)
    result = lax.map(one_head, (query_heads, key_heads, value_heads))
    return jnp.transpose(result, (1, 0, 2)).reshape(WINDOW_TOKENS, HEADS * DH)

def reference(query_lin, key_lin, value_lin, log_decay, out_gate, norm_gain, state_in, query_soft, key_soft, value_soft):
    queries = jax.nn.silu(query_lin.astype(jnp.float32)).astype(jnp.bfloat16).reshape(WINDOW_TOKENS, LHEADS, DH)
    keys_act = (jax.nn.silu(key_lin.astype(jnp.float32)) * DH ** (-0.5)).astype(jnp.bfloat16).reshape(WINDOW_TOKENS, LHEADS, DH)
    values = value_lin.reshape(WINDOW_TOKENS, LHEADS, DH)
    decays = log_decay.astype(jnp.float32)
    mixed_heads, state_out = lightning_blocks(queries, keys_act, values, decays, state_in, BLK)
    light_out = finish_rows(mixed_heads.reshape(WINDOW_TOKENS, LHEADS * DH), out_gate, norm_gain)
    attn_out = soft_attention(query_soft, key_soft, value_soft)
    return (light_out, state_out, attn_out)
```

```python
import functools
import math

import jax
import jax.numpy as jnp
from jax import lax
from jax.experimental import pallas as pl
from jax.experimental.pallas import tpu as pltpu
from jax.sharding import PartitionSpec as P

DH = 128
NZ = 8
LHEADS = 32
NORM_EPS = 1e-6
SCALE = DH ** (-0.5)
EXP2_SCALE = SCALE * math.log2(math.e)
MASKED = -1e30
MESH = pl.DeviceIdType.MESH
F32 = jnp.float32
BF16 = jnp.bfloat16
ROWS_BY_ROWS = (((1,), (1,)), ((), ()))
COLS_BY_COLS = (((0,), (0,)), ((), ()))
Z_ORDER = (4, 3, 5, 2, 6, 1, 7)


def place(x, z, c):
    return (x * NZ + z) * 2 + c


def block(index):
    return pl.ds(pl.multiple_of(index * DH, DH), DH)


def wide(index, width):
    return pl.ds(pl.multiple_of(index * width, width), width)


def kernel(
    ql_in, kl_in, vl_in, ld_in, gate_in, gain_in, state_in, q_in, k_in, v_in,
    light_out, state_out, attn_out,
    kv, qx, qs, acc, top, low, ob,
    qlv, klv, vlv, gtv, lin, ct, cv, s_own, s_oth, s_par, ssend, sgot, eout, egot, ent, esend,
    stin, t0, fin, dt, chd, sq,
    lsem, kvs, kvr, qsend, qrecv, st_s, st_r, d_s, d_r, sp_s, sp_r, cd_s, cd_r, sa_s, sa_r,
    eo_s, eo_r, t_s, t_r, so_s, so_r, ep_s, ep_r, ag_s, ag_r, o_s, o_r, out_s,
):
    me = lax.axis_index("seq")
    x = me // (2 * NZ)
    z = (me // 2) % NZ
    c = me % 2
    quad = x * 2 + c
    mates = {1: (x, 1 - c), 2: (1 - x, c), 3: (1 - x, 1 - c)}

    def mate_quad(p):
        mx, mc = mates[p]
        return mx * 2 + mc

    def mate_at(p):
        mx, mc = mates[p]
        return place(mx, z, mc)

    def up(k):
        return (z + k) % NZ

    def remote(src, dst, send, recv, to):
        return pltpu.make_async_remote_copy(
            src_ref=src, dst_ref=dst, send_sem=send, recv_sem=recv,
            device_id={"seq": to}, device_id_type=MESH,
        )

    sends = []

    def go(copy):
        copy.start()
        sends.append(copy)

    barrier = pltpu.get_barrier_semaphore()
    peers = [mate_at(p) for p in (1, 2, 3)] + [place(x, up(k), c) for k in range(1, NZ)]
    for peer in peers:
        pl.semaphore_signal(barrier, inc=1, device_id={"seq": peer}, device_id_type=MESH)

    loads = [
        pltpu.make_async_copy(kl_in, klv, lsem.at[0]),
        pltpu.make_async_copy(vl_in, vlv, lsem.at[1]),
        pltpu.make_async_copy(ql_in, qlv, lsem.at[2]),
        pltpu.make_async_copy(gate_in, gtv, lsem.at[3]),
    ]
    for load in loads:
        load.start()

    def head_of(n, parity):
        return 16 * (n % 2) + 2 * (n // 2) + parity

    t_row = lax.broadcasted_iota(jnp.int32, (DH, DH), 0)
    t_col = lax.broadcasted_iota(jnp.int32, (DH, DH), 1)
    tril = jnp.where(t_row >= t_col, 1.0, 0.0).astype(BF16)
    cum = jnp.dot(tril, ld_in[...], preferred_element_type=F32)
    cv[...] = cum
    cum_t = jnp.transpose(cum)
    ct[...] = cum_t
    dt[c] = jnp.broadcast_to(cum_t[:, DH - 1 :], (LHEADS, DH))

    pl.semaphore_wait(barrier, len(peers))

    def kv_quad(hh, sel, p):
        src_all = (k_in, v_in)[sel]
        head = mate_quad(p) * 2 + hh
        return remote(
            src_all.at[:, block(head)], kv.at[z, hh, sel, block(quad), :],
            kvs.at[hh, sel, p], kvr.at[hh, sel, p], mate_at(p),
        )

    def kv_own(hh, sel):
        src_all = (k_in, v_in)[sel]
        return pltpu.make_async_copy(
            src_all.at[:, block(quad * 2 + hh)], kv.at[z, hh, sel, block(quad), :], kvr.at[hh, sel, 0]
        )

    def q_quad(p):
        return remote(
            q_in.at[:, wide(mate_quad(p), 1024)], qx.at[quad], qsend.at[p], qrecv.at[p], mate_at(p)
        )

    q_own = pltpu.make_async_copy(q_in.at[:, wide(quad, 1024)], qx.at[quad], qrecv.at[0])
    for hh in range(2):
        for p in (2, 3, 1):
            for sel in range(2):
                go(kv_quad(hh, sel, p))
        for sel in range(2):
            kv_own(hh, sel).start()
    go(remote(dt.at[c], dt.at[c], d_s, d_r, mate_at(1)))

    st_own = pltpu.make_async_copy(state_in.at[0], stin.at[0], st_r.at[0])
    st_move = remote(state_in.at[0], stin.at[1], st_s, st_r.at[1], mate_at(2))

    @pl.when(x == 0)
    def _():
        st_own.start()

    @pl.when(x == 1)
    def _():
        st_move.start()

    for p in (2, 3, 1):
        go(q_quad(p))
    q_own.start()

    def column(h):
        lanes = lax.broadcasted_iota(jnp.int32, (DH, LHEADS), 1)
        return jnp.sum(jnp.where(lanes == h, cv[...], 0.0), axis=1, keepdims=True)

    def silu(u):
        return u / (1.0 + jnp.exp(-u))

    def block_states(parity, target):
        def step(n, carry):
            h = head_of(n, parity)
            keys = (silu(klv[:, block(h)].astype(F32)) * SCALE).astype(BF16)
            klv[:, block(h)] = keys
            col = column(h)
            decayed = (keys.astype(F32) * jnp.exp(col[DH - 1 :, :] - col)).astype(BF16)
            state = lax.dot_general(
                decayed, vlv[:, block(h)], COLS_BY_COLS, preferred_element_type=F32
            )
            target[n] = state.astype(target.dtype)
            return carry

        lax.fori_loop(0, 16, step, 0, unroll=2)

    loads[0].wait()
    loads[1].wait()
    block_states(1 - c, s_oth)
    go(remote(s_oth, s_par, sp_s, sp_r, mate_at(1)))
    block_states(c, s_own)

    def ring(hh, way, step):
        slot = (z + (NZ - step if way == 0 else step)) % NZ
        to = place(x, up(1 if way == 0 else NZ - 1), c)
        return remote(
            kv.at[slot, hh], kv.at[slot, hh], ag_s.at[hh, way, step], ag_r.at[hh, way, step], to
        )

    def ring_got(hh, way, distance):
        slot = (z + (NZ - distance if way == 0 else distance)) % NZ
        to = place(x, up(1 if way == 0 else NZ - 1), c)
        return remote(
            kv.at[slot, hh], kv.at[slot, hh],
            ag_s.at[hh, way, distance - 1], ag_r.at[hh, way, distance - 1], to,
        )

    def reach(hh, way):
        return 4 if way == hh else 3

    def start_ring(hh):
        for sel in range(2):
            kv_own(hh, sel).wait()
            for p in (1, 2, 3):
                kv_quad(hh, sel, p).wait_recv()
        for way in range(2):
            go(ring(hh, way, 0))

    start_ring(0)

    remote(dt.at[c], dt.at[c], d_s, d_r, mate_at(1)).wait_recv()
    remote(s_oth, s_par, sp_s, sp_r, mate_at(1)).wait_recv()
    first = c == 0
    chd[z] = dt[0] + dt[1]

    def chip_state(n, carry):
        h = head_of(n, c)
        later = jnp.exp(dt[1, pl.ds(h, 1), :])
        own, par = s_own[n], s_par[n].astype(F32)
        earlier_state = jnp.where(first, own, par)
        later_state = jnp.where(first, par, own)
        ssend[n // 2, n % 2] = (later * earlier_state + later_state).astype(BF16)
        s_own[n] = earlier_state
        return carry

    lax.fori_loop(0, 16, chip_state, 0, unroll=2)
    sgot[z] = ssend[z]

    def chip_decay(k):
        return remote(chd.at[z], chd.at[z], cd_s.at[k - 1], cd_r.at[k - 1], place(x, up(k), c))

    def chip_decay_got(k):
        slot = up(NZ - k)
        return remote(chd.at[slot], chd.at[slot], cd_s.at[k - 1], cd_r.at[k - 1], place(x, up(k), c))

    def state_move(k):
        return remote(
            ssend.at[up(k)], sgot.at[z], sa_s.at[k - 1], sa_r.at[k - 1], place(x, up(k), c)
        )

    def state_got(k):
        return remote(
            ssend.at[up(k)], sgot.at[up(NZ - k)], sa_s.at[k - 1], sa_r.at[k - 1], place(x, up(k), c)
        )

    for k in Z_ORDER:
        go(chip_decay(k))
        go(state_move(k))

    q_own.wait()
    for p in (1, 2, 3):
        q_quad(p).wait_recv()
    for qb in range(4):
        for hh in range(2):
            for j in range(4):
                qs[hh, qb // 2, j, (qb % 2) * DH : (qb % 2 + 1) * DH, :] = qx[
                    qb, :, (hh * 4 + j) * DH : (hh * 4 + j + 1) * DH
                ]

    start_ring(1)

    def attend(hh, half, j, slot, keys, own):
        s = lax.dot_general(
            qs[hh, half, j], kv[slot, hh, 0, 0:keys, :], ROWS_BY_ROWS, preferred_element_type=F32
        )
        if own:
            row = lax.broadcasted_iota(jnp.int32, (2 * DH, keys), 0)
            col = lax.broadcasted_iota(jnp.int32, (2 * DH, keys), 1)
            s = jnp.where(row >= col - (keys - 2 * DH), s, MASKED)
        now = jnp.max(s, axis=1, keepdims=True)
        if own:
            new = jnp.broadcast_to(now, (2 * DH, DH))
        else:
            old = top[half, j]
            new = jnp.maximum(old, now)
        spread = jnp.concatenate([new] * (keys // DH), axis=1)
        raised = jnp.exp2((s - spread) * EXP2_SCALE)
        part = raised[:, 0:DH]
        for i in range(1, keys // DH):
            part = part + raised[:, i * DH : (i + 1) * DH]
        summed = jnp.dot(
            raised.astype(BF16), kv[slot, hh, 1, 0:keys, :], preferred_element_type=F32
        )
        if own:
            low[half, j] = part
            acc[half, j] = summed
        else:
            fade = jnp.exp2((old - new) * EXP2_SCALE)
            low[half, j] = low[half, j] * fade + part
            acc[half, j] = acc[half, j] * fade + summed
        top[half, j] = new

    def own_slot(hh):
        def step(j, carry):
            attend(hh, 0, j, z, 2 * DH, True)
            attend(hh, 1, j, z, 4 * DH, True)
            return carry

        lax.fori_loop(0, 4, step, 0)

    def other_slot(hh, slot):
        @pl.when(slot < z)
        def _():
            def step(j, carry):
                attend(hh, 0, j, slot, 2 * DH, False)
                attend(hh, 1, j, slot, 4 * DH, False)
                return carry

            lax.fori_loop(0, 4, step, 0)

        @pl.when(slot > z)
        def _():
            def step(j, carry):
                attend(hh, 1, j, slot, 2 * DH, False)
                return carry

            lax.fori_loop(0, 4, step, 0)

    def ring_step(hh, distance):
        ways = [way for way in range(2) if distance <= reach(hh, way)]
        for way in ways:
            ring_got(hh, way, distance).wait_recv()
            if distance < reach(hh, way):
                go(ring(hh, way, distance))
        if len(ways) == 2:
            def step(way, carry):
                other_slot(hh, (z + NZ - distance + 2 * distance * way) % NZ)
                return carry

            lax.fori_loop(0, 2, step, 0)
        else:
            other_slot(hh, (z + (NZ - distance if ways[0] == 0 else distance)) % NZ)

    def finish_heads(hh):
        for half in range(2):
            def step(j, carry):
                total = jnp.sum(low[half, j], axis=1, keepdims=True)
                result = (acc[half, j] / total).astype(BF16)
                ob[hh, 2 * half, :, block(j)] = result[0:DH]
                ob[hh, 2 * half + 1, :, block(j)] = result[DH:]
                return carry

            lax.fori_loop(0, 4, step, 0)
        for p in (2, 3, 1):
            go(out_quad(hh, p))
        out_own(hh).start()

    def out_quad(hh, p):
        return remote(
            ob.at[hh, mate_quad(p)], attn_out.at[:, wide(quad * 2 + hh, 512)],
            o_s.at[hh, p], o_r.at[hh, p], mate_at(p),
        )

    def out_got(hh, p):
        return remote(
            ob.at[hh, mate_quad(p)], attn_out.at[:, wide(mate_quad(p) * 2 + hh, 512)],
            o_s.at[hh, p], o_r.at[hh, p], mate_at(p),
        )

    def out_own(hh):
        return pltpu.make_async_copy(
            ob.at[hh, quad], attn_out.at[:, wide(quad * 2 + hh, 512)], o_r.at[hh, 0]
        )

    def inner_heads():
        def step(h, carry):
            queries = silu(qlv[:, block(h)].astype(F32)).astype(BF16)
            qlv[:, block(h)] = queries
            scores = lax.dot_general(
                queries, klv[:, block(h)], ROWS_BY_ROWS, preferred_element_type=F32
            )
            spread = column(h) - ct[pl.ds(h, 1), :]
            damping = jnp.exp(jnp.where(t_row >= t_col, spread, MASKED))
            damped = (scores * damping).astype(BF16)
            lin[:, block(h)] = jnp.dot(damped, vlv[:, block(h)], preferred_element_type=F32)
            return carry

        lax.fori_loop(0, LHEADS, step, 0, unroll=2)

    t_move = remote(fin, t0, t_s, t_r, mate_at(2))
    so_move = remote(fin.at[0], state_out.at[0], so_s, so_r.at[0], mate_at(2))
    so_own = pltpu.make_async_copy(fin.at[1], state_out.at[0], so_r.at[1])

    def enter_move(k):
        return remote(eout.at[up(k)], egot.at[z], eo_s.at[k - 1], eo_r.at[k - 1], place(x, up(k), c))

    def enter_got(k):
        return remote(
            eout.at[up(k)], egot.at[up(NZ - k)], eo_s.at[k - 1], eo_r.at[k - 1], place(x, up(k), c)
        )

    def owner():
        for k in Z_ORDER:
            chip_decay_got(k).wait_recv()
            state_got(k).wait_recv()

        @pl.when(x == 0)
        def _():
            st_own.wait()
            st_move.wait_recv()
            fin[...] = stin[...]

        @pl.when(x == 1)
        def _():
            t_move.wait_recv()
            fin[...] = t0[...]

        for k in range(2):
            state = fin[k]
            for zi in range(NZ):
                eout[zi, k] = state.astype(BF16)
                decay = jnp.exp(chd[zi, pl.ds(16 * k + 2 * z + c, 1), :])
                state = decay * state + sgot[zi, k].astype(F32)
            fin[k] = state

        @pl.when(x == 0)
        def _():
            t_move.start()

        @pl.when(x == 1)
        def _():
            so_move.start()
            so_own.start()

        for k in Z_ORDER:
            go(enter_move(k))
        egot[z] = eout[z]

    def pair_enter():
        for k in Z_ORDER:
            enter_got(k).wait_recv()

        def step(n, carry):
            h = head_of(n, c)
            entering = egot[n // 2, n % 2]
            after = (jnp.exp(dt[0, pl.ds(h, 1), :]) * entering.astype(F32) + s_own[n]).astype(BF16)
            ent[c, n] = jnp.where(first, entering, after)
            esend[n] = jnp.where(first, after, entering)
            return carry

        lax.fori_loop(0, 16, step, 0, unroll=2)
        go(enter_pair)

    enter_pair = remote(esend, ent.at[c], ep_s, ep_r, mate_at(1))
    enter_pair_got = remote(esend, ent.at[1 - c], ep_s, ep_r, mate_at(1))

    def lightning_end():
        sq[...] = jnp.zeros_like(sq)

        def carried(parity):
            def step(n, carry):
                h = head_of(n, parity)
                reached = jnp.dot(qlv[:, block(h)], ent[parity, n], preferred_element_type=F32)
                mixed = lin[:, block(h)] + jnp.exp(column(h)) * reached
                lin[:, block(h)] = mixed
                sq[...] += mixed * mixed
                return carry

            lax.fori_loop(0, 16, step, 0, unroll=2)

        carried(c)
        enter_pair_got.wait_recv()
        carried(1 - c)
        mean = jnp.sum(sq[...], axis=1, keepdims=True) / (LHEADS * DH)
        factor = jnp.broadcast_to(lax.rsqrt(mean + NORM_EPS), (DH, DH))

        def gated(h, carry):
            gate = 1.0 / (1.0 + jnp.exp(-gtv[:, block(h)].astype(F32)))
            row = lin[:, block(h)] * factor * gain_in[:, block(h)] * gate
            qlv[:, block(h)] = row.astype(BF16)
            return carry

        lax.fori_loop(0, LHEADS, gated, 0, unroll=2)
        light_copy.start()

    light_copy = pltpu.make_async_copy(qlv, light_out, out_s)

    own_slot(0)
    ring_step(0, 1)
    loads[2].wait()
    inner_heads()
    ring_step(0, 2)
    owner()
    ring_step(0, 3)
    ring_step(0, 4)
    finish_heads(0)
    own_slot(1)
    ring_step(1, 1)
    ring_step(1, 2)
    pair_enter()
    ring_step(1, 3)
    loads[3].wait()
    lightning_end()
    ring_step(1, 4)
    finish_heads(1)

    for hh in range(2):
        out_own(hh).wait()
        for p in (1, 2, 3):
            out_got(hh, p).wait_recv()
    light_copy.wait()

    @pl.when(x == 0)
    def _():
        so_move.wait_recv()
        t_move.wait_send()

    @pl.when(x == 1)
    def _():
        st_move.wait_send()
        so_own.wait()
        so_move.wait_send()

    for copy in sends:
        copy.wait_send()


def shards(*arrays):
    (query_lin, key_lin, value_lin, log_decay, out_gate, norm_gain, state_in, query_soft, key_soft,
     value_soft) = arrays
    rows, width = query_lin.shape
    hbm = pl.BlockSpec(memory_space=pl.ANY)
    vmem = pl.BlockSpec(memory_space=pltpu.VMEM)
    dma = pltpu.SemaphoreType.DMA
    state = (DH, DH)
    return pl.pallas_call(
        kernel,
        out_shape=(
            jax.ShapeDtypeStruct((rows, width), BF16),
            jax.ShapeDtypeStruct(state_in.shape, F32),
            jax.ShapeDtypeStruct((rows, width), BF16),
        ),
        in_specs=[hbm, hbm, hbm, vmem, hbm, vmem, hbm, hbm, hbm, hbm],
        out_specs=(hbm, hbm, hbm),
        scratch_shapes=[
            pltpu.VMEM((NZ, 2, 2, 512, DH), BF16),
            pltpu.VMEM((4, rows, 1024), BF16),
            pltpu.VMEM((2, 2, 4, 256, DH), BF16),
            pltpu.VMEM((2, 4, 256, DH), F32),
            pltpu.VMEM((2, 4, 256, DH), F32),
            pltpu.VMEM((2, 4, 256, DH), F32),
            pltpu.VMEM((2, 4, rows, 512), BF16),
            pltpu.VMEM((rows, width), BF16),
            pltpu.VMEM((rows, width), BF16),
            pltpu.VMEM((rows, width), BF16),
            pltpu.VMEM((rows, width), BF16),
            pltpu.VMEM((rows, width), F32),
            pltpu.VMEM((LHEADS, DH), F32),
            pltpu.VMEM((DH, LHEADS), F32),
            pltpu.VMEM((16,) + state, F32),
            pltpu.VMEM((16,) + state, BF16),
            pltpu.VMEM((16,) + state, BF16),
            pltpu.VMEM((NZ, 2) + state, BF16),
            pltpu.VMEM((NZ, 2) + state, BF16),
            pltpu.VMEM((NZ, 2) + state, BF16),
            pltpu.VMEM((NZ, 2) + state, BF16),
            pltpu.VMEM((2, 16) + state, BF16),
            pltpu.VMEM((16,) + state, BF16),
            pltpu.VMEM((2,) + state, F32),
            pltpu.VMEM((2,) + state, F32),
            pltpu.VMEM((2,) + state, F32),
            pltpu.VMEM((2, LHEADS, DH), F32),
            pltpu.VMEM((NZ, LHEADS, DH), F32),
            pltpu.VMEM(state, F32),
            dma((4,)),
            dma((2, 2, 4)), dma((2, 2, 4)),
            dma((4,)), dma((4,)),
            dma, dma((2,)),
            dma, dma,
            dma, dma,
            dma((7,)), dma((7,)),
            dma((7,)), dma((7,)),
            dma((7,)), dma((7,)),
            dma, dma,
            dma, dma((2,)),
            dma, dma,
            dma((2, 2, 4)), dma((2, 2, 4)),
            dma((2, 4)), dma((2, 4)),
            dma,
        ],
        compiler_params=pltpu.CompilerParams(
            collective_id=0, has_side_effects=True, vmem_limit_bytes=48 * 2**20
        ),
        name="window",
    )(
        query_lin, key_lin, value_lin, log_decay, out_gate, norm_gain.reshape(1, width), state_in,
        query_soft, key_soft, value_soft,
    )


def solution(mesh):
    rows = P(("dp", "seq"), None)
    states = P(("dp", "seq"), None, None)
    return jax.shard_map(
        shards,
        mesh=mesh,
        in_specs=(rows, rows, rows, rows, rows, P(), states, rows, rows, rows),
        out_specs=(rows, states, rows),
        check_vma=False,
    )
```

```python
import functools
import math

import jax
import jax.numpy as jnp
from jax import lax
from jax.experimental import pallas as pl
from jax.experimental.pallas import tpu as pltpu
from jax.sharding import PartitionSpec as P

DH = 128
NZ = 8
LHEADS = 32
NORM_EPS = 1e-6
SCALE = DH ** (-0.5)
EXP2_SCALE = SCALE * math.log2(math.e)
MASKED = -1e30
MESH = pl.DeviceIdType.MESH
F32 = jnp.float32
BF16 = jnp.bfloat16
UNROLL = 4
ROWS_BY_ROWS = (((1,), (1,)), ((), ()))
COLS_BY_COLS = (((0,), (0,)), ((), ()))
Z_ORDER = (4, 3, 5, 2, 6, 1, 7)


def place(x, z, c):
    return (x * NZ + z) * 2 + c


def block(index):
    return pl.ds(pl.multiple_of(index * DH, DH), DH)


def wide(index, width):
    return pl.ds(pl.multiple_of(index * width, width), width)


def kernel(
    ql_in, kl_in, vl_in, ld_in, gate_in, gain_in, state_in, q_in, k_in, v_in,
    light_out, state_out, attn_out,
    kv, qx, acc, top, low, ob, vsv, vtl,
    qlv, klv, vlv, gtv, lin, ct, cv, s_own, s_oth, s_par, ssend, sgot, eout, egot, ent, esend, gf,
    stin, t0, fin, dt, chd, sq,
    lsem, kvs, kvr, qsend, qrecv, st_s, st_r, d_s, d_r, sp_s, sp_r, cd_s, cd_r, sa_s, sa_r,
    eo_s, eo_r, t_s, t_r, so_s, so_r, ep_s, ep_r, ag_s, ag_r, o_s, o_r, out_s,
):
    me = lax.axis_index("seq")
    x = me // (2 * NZ)
    z = (me // 2) % NZ
    c = me % 2
    quad = x * 2 + c
    mates = {1: (x, 1 - c), 2: (1 - x, c), 3: (1 - x, 1 - c)}

    def mate_quad(p):
        mx, mc = mates[p]
        return mx * 2 + mc

    def mate_at(p):
        mx, mc = mates[p]
        return place(mx, z, mc)

    def up(k):
        return (z + k) % NZ

    def remote(src, dst, send, recv, to):
        return pltpu.make_async_remote_copy(
            src_ref=src, dst_ref=dst, send_sem=send, recv_sem=recv,
            device_id={"seq": to}, device_id_type=MESH,
        )

    sends = []

    def go(copy):
        copy.start()
        sends.append(copy)

    barrier = pltpu.get_barrier_semaphore()
    peers = [mate_at(p) for p in (1, 2, 3)] + [place(x, up(k), c) for k in range(1, NZ)]
    for peer in peers:
        pl.semaphore_signal(barrier, inc=1, device_id={"seq": peer}, device_id_type=MESH)

    loads = [
        pltpu.make_async_copy(v_in, vsv, lsem.at[0]),
        pltpu.make_async_copy(kl_in, klv, lsem.at[1]),
        pltpu.make_async_copy(vl_in, vlv, lsem.at[2]),
        pltpu.make_async_copy(ql_in, qlv, lsem.at[3]),
        pltpu.make_async_copy(gate_in, gtv, lsem.at[4]),
    ]
    for load in loads:
        load.start()

    def head_of(n, parity):
        return 16 * (n % 2) + 2 * (n // 2) + parity

    t_row = lax.broadcasted_iota(jnp.int32, (DH, DH), 0)
    t_col = lax.broadcasted_iota(jnp.int32, (DH, DH), 1)
    tril = jnp.where(t_row >= t_col, 1.0, 0.0).astype(BF16)
    cum = jnp.dot(tril, ld_in[...], preferred_element_type=F32)
    cv[...] = cum
    cum_t = jnp.transpose(cum)
    ct[...] = cum_t
    dt[c] = jnp.broadcast_to(cum_t[:, DH - 1 :], (LHEADS, DH))

    loads[0].wait()
    for g in range(8):
        vtl[g] = jnp.transpose(vsv[:, g * DH : (g + 1) * DH])

    pl.semaphore_wait(barrier, len(peers))

    def kv_quad(hh, sel, p):
        head = mate_quad(p) * 2 + hh
        src = vtl.at[head] if sel else k_in.at[:, block(head)]
        return remote(
            src, kv.at[z, hh, x, sel, block(c), :], kvs.at[hh, sel, p], kvr.at[hh, sel, p], mate_at(p)
        )

    def kv_quad_got(hh, sel, p):
        head = mate_quad(p) * 2 + hh
        src = vtl.at[head] if sel else k_in.at[:, block(head)]
        mx, mc = mates[p]
        return remote(
            src, kv.at[z, hh, mx, sel, block(mc), :], kvs.at[hh, sel, p], kvr.at[hh, sel, p], mate_at(p)
        )

    def kv_own(hh, sel):
        head = quad * 2 + hh
        src = vtl.at[head] if sel else k_in.at[:, block(head)]
        return pltpu.make_async_copy(src, kv.at[z, hh, x, sel, block(c), :], kvr.at[hh, sel, 0])

    for hh in range(2):
        for sel in range(2):
            go(kv_quad(hh, sel, 1))
            kv_own(hh, sel).start()
    for hh in range(2):
        for p in (2, 3):
            for sel in range(2):
                go(kv_quad(hh, sel, p))
    go(remote(dt.at[c], dt.at[c], d_s, d_r, mate_at(1)))

    def ring(hh, way, step, half):
        slot = (z + (NZ - step if way == 0 else step)) % NZ
        to = place(x, up(1 if way == 0 else NZ - 1), c)
        piece = kv.at[slot, hh, x if half == 0 else 1 - x]
        return remote(piece, piece, ag_s.at[hh, way, step, half], ag_r.at[hh, way, step, half], to)

    def ring_got(hh, way, distance, half):
        slot = (z + (NZ - distance if way == 0 else distance)) % NZ
        to = place(x, up(1 if way == 0 else NZ - 1), c)
        piece = kv.at[slot, hh, x if half == 0 else 1 - x]
        step = distance - 1
        return remote(piece, piece, ag_s.at[hh, way, step, half], ag_r.at[hh, way, step, half], to)

    def reach(hh, way):
        return 4 if way == hh else 3

    def start_ring(hh, half):
        for sel in range(2):
            if half == 0:
                kv_own(hh, sel).wait()
                kv_quad_got(hh, sel, 1).wait_recv()
            else:
                kv_quad_got(hh, sel, 2).wait_recv()
                kv_quad_got(hh, sel, 3).wait_recv()
        for way in range(2):
            go(ring(hh, way, 0, half))

    def pump(hh, distance):
        for half in range(2):
            for way in range(2):
                if distance <= reach(hh, way):
                    ring_got(hh, way, distance, half).wait_recv()
                    if distance < reach(hh, way):
                        go(ring(hh, way, distance, half))

    def column(h):
        lanes = lax.broadcasted_iota(jnp.int32, (DH, LHEADS), 1)
        return jnp.sum(jnp.where(lanes == h, cv[...], 0.0), axis=1, keepdims=True)

    def silu(u):
        return u / (1.0 + jnp.exp(-u))

    def block_states(parity, target):
        def step(n, carry):
            h = head_of(n, parity)
            keys = (silu(klv[:, block(h)].astype(F32)) * SCALE).astype(BF16)
            klv[:, block(h)] = keys
            col = column(h)
            decayed = (keys.astype(F32) * jnp.exp(col[DH - 1 :, :] - col)).astype(BF16)
            state = lax.dot_general(
                decayed, vlv[:, block(h)], COLS_BY_COLS, preferred_element_type=F32
            )
            target[n] = state.astype(target.dtype)
            return carry

        lax.fori_loop(0, 16, step, 0, unroll=4)

    start_ring(0, 0)
    start_ring(1, 0)
    loads[1].wait()
    loads[2].wait()
    block_states(1 - c, s_oth)
    go(remote(s_oth, s_par, sp_s, sp_r, mate_at(1)))
    start_ring(0, 1)
    block_states(c, s_own)
    start_ring(1, 1)

    def q_quad(hh, p):
        return remote(
            q_in.at[:, wide(mate_quad(p) * 2 + hh, 512)], qx.at[hh, quad],
            qsend.at[hh, p], qrecv.at[hh, p], mate_at(p),
        )

    def q_quad_got(hh, p):
        return remote(
            q_in.at[:, wide(mate_quad(p) * 2 + hh, 512)], qx.at[hh, mate_quad(p)],
            qsend.at[hh, p], qrecv.at[hh, p], mate_at(p),
        )

    def q_own(hh):
        return pltpu.make_async_copy(
            q_in.at[:, wide(quad * 2 + hh, 512)], qx.at[hh, quad], qrecv.at[hh, 0]
        )

    for hh in range(2):
        for p in (2, 3, 1):
            go(q_quad(hh, p))
        q_own(hh).start()

    st_own = pltpu.make_async_copy(state_in.at[0], stin.at[0], st_r.at[0])
    st_move = remote(state_in.at[0], stin.at[1], st_s, st_r.at[1], mate_at(2))

    @pl.when(x == 0)
    def _():
        st_own.start()

    @pl.when(x == 1)
    def _():
        st_move.start()

    remote(dt.at[c], dt.at[1 - c], d_s, d_r, mate_at(1)).wait_recv()
    remote(s_oth, s_par, sp_s, sp_r, mate_at(1)).wait_recv()
    first = c == 0
    chd[z] = dt[0] + dt[1]

    def chip_state(n, carry):
        h = head_of(n, c)
        later = jnp.exp(dt[1, pl.ds(h, 1), :])
        own, par = s_own[n], s_par[n].astype(F32)
        earlier_state = jnp.where(first, own, par)
        later_state = jnp.where(first, par, own)
        ssend[n // 2, n % 2] = (later * earlier_state + later_state).astype(BF16)
        s_own[n] = earlier_state
        return carry

    lax.fori_loop(0, 16, chip_state, 0, unroll=2)
    sgot[z] = ssend[z]

    def chip_decay(k):
        return remote(chd.at[z], chd.at[z], cd_s.at[k - 1], cd_r.at[k - 1], place(x, up(k), c))

    def chip_decay_got(k):
        slot = up(NZ - k)
        return remote(chd.at[slot], chd.at[slot], cd_s.at[k - 1], cd_r.at[k - 1], place(x, up(k), c))

    def state_move(k):
        return remote(
            ssend.at[up(k)], sgot.at[z], sa_s.at[k - 1], sa_r.at[k - 1], place(x, up(k), c)
        )

    def state_got(k):
        return remote(
            ssend.at[up(k)], sgot.at[up(NZ - k)], sa_s.at[k - 1], sa_r.at[k - 1], place(x, up(k), c)
        )

    for k in Z_ORDER:
        go(chip_decay(k))
        go(state_move(k))

    def attend(hh, half, j, slot, both, own):
        heads = pl.ds(pl.multiple_of(j * DH, DH), DH)
        queries = jnp.concatenate([qx[hh, 2 * half, :, heads], qx[hh, 2 * half + 1, :, heads]], axis=0)
        parts = (0, 1) if both else (0,)
        keys = jnp.concatenate([kv[slot, hh, i, 0] for i in parts], axis=0)
        values = jnp.concatenate(
            [kv[slot, hh, i, 1, b * DH : (b + 1) * DH, :] for i in parts for b in range(2)], axis=1
        )
        s = lax.dot_general(keys, queries, ROWS_BY_ROWS, preferred_element_type=F32)
        if own:
            count = s.shape[0]
            key = lax.broadcasted_iota(jnp.int32, s.shape, 0) - (count - 2 * DH)
            query = lax.broadcasted_iota(jnp.int32, s.shape, 1)
            s = jnp.where(key <= query, s, MASKED)
        row = pl.ds(half * 4 + j, 1)
        new = jnp.max(s, axis=0, keepdims=True)
        if not own:
            old = top[hh, row, :]
            new = jnp.maximum(old, new)
        raised = jnp.exp2((s - new) * EXP2_SCALE)
        part = jnp.sum(raised, axis=0, keepdims=True)
        summed = jnp.dot(values, raised.astype(BF16), preferred_element_type=F32)
        if own:
            low[hh, row, :] = part
            acc[hh, half, j] = summed
        else:
            fade = jnp.exp2((old - new) * EXP2_SCALE)
            low[hh, row, :] = low[hh, row, :] * fade + part
            acc[hh, half, j] = acc[hh, half, j] * fade + summed
        top[hh, row, :] = new

    def over_heads(body):
        def step(j, carry):
            body(j)
            return carry

        lax.fori_loop(0, 4, step, 0, unroll=UNROLL)

    def own_slot(hh):
        def body(j):
            attend(hh, 0, j, z, False, True)
            attend(hh, 1, j, z, True, True)

        over_heads(body)

    def other_slot(hh, slot):
        @pl.when(slot < z)
        def _():
            def body(j):
                attend(hh, 0, j, slot, False, False)
                attend(hh, 1, j, slot, True, False)

            over_heads(body)

        @pl.when(slot > z)
        def _():
            over_heads(lambda j: attend(hh, 1, j, slot, False, False))

    def process(hh, distance):
        ways = [way for way in range(2) if distance <= reach(hh, way)]
        if len(ways) == 2:
            def step(way, carry):
                other_slot(hh, (z + NZ - distance + 2 * distance * way) % NZ)
                return carry

            lax.fori_loop(0, 2, step, 0)
        else:
            other_slot(hh, (z + (NZ - distance if ways[0] == 0 else distance)) % NZ)

    def finish_heads(hh):
        for half in range(2):
            def step(j, carry):
                scale = 1.0 / low[hh, pl.ds(half * 4 + j, 1), :]
                result = jnp.transpose(acc[hh, half, j] * scale).astype(BF16)
                ob[hh, 2 * half, :, block(j)] = result[0:DH]
                ob[hh, 2 * half + 1, :, block(j)] = result[DH:]
                return carry

            lax.fori_loop(0, 4, step, 0, unroll=2)
        for p in (2, 3, 1):
            go(out_quad(hh, p))
        out_own(hh).start()

    def out_quad(hh, p):
        return remote(
            ob.at[hh, mate_quad(p)], attn_out.at[:, wide(quad * 2 + hh, 512)],
            o_s.at[hh, p], o_r.at[hh, p], mate_at(p),
        )

    def out_got(hh, p):
        return remote(
            ob.at[hh, mate_quad(p)], attn_out.at[:, wide(mate_quad(p) * 2 + hh, 512)],
            o_s.at[hh, p], o_r.at[hh, p], mate_at(p),
        )

    def out_own(hh):
        return pltpu.make_async_copy(
            ob.at[hh, quad], attn_out.at[:, wide(quad * 2 + hh, 512)], o_r.at[hh, 0]
        )

    def queries_here(hh):
        q_own(hh).wait()
        for p in (1, 2, 3):
            q_quad_got(hh, p).wait_recv()

    def inner_heads(begin, end):
        def step(h, carry):
            queries = silu(qlv[:, block(h)].astype(F32)).astype(BF16)
            qlv[:, block(h)] = queries
            scores = lax.dot_general(
                queries, klv[:, block(h)], ROWS_BY_ROWS, preferred_element_type=F32
            )
            spread = column(h) - ct[pl.ds(h, 1), :]
            damping = jnp.exp(jnp.where(t_row >= t_col, spread, MASKED))
            damped = (scores * damping).astype(BF16)
            lin[:, block(h)] = jnp.dot(damped, vlv[:, block(h)], preferred_element_type=F32)
            return carry

        lax.fori_loop(begin, end, step, 0, unroll=4)

    t_move = remote(fin, t0, t_s, t_r, mate_at(2))
    so_move = remote(fin.at[0], state_out.at[0], so_s, so_r.at[0], mate_at(2))
    so_own = pltpu.make_async_copy(fin.at[1], state_out.at[0], so_r.at[1])

    def enter_move(k, part):
        return remote(
            eout.at[up(k), part], egot.at[z, part],
            eo_s.at[part, k - 1], eo_r.at[part, k - 1], place(x, up(k), c),
        )

    def enter_got(k, part):
        return remote(
            eout.at[up(k), part], egot.at[up(NZ - k), part],
            eo_s.at[part, k - 1], eo_r.at[part, k - 1], place(x, up(k), c),
        )

    def prefix():
        for k in range(2):
            state = fin[k]
            for zi in range(NZ):
                eout[zi, k] = state.astype(BF16)
                decay = jnp.exp(chd[zi, pl.ds(16 * k + 2 * z + c, 1), :])
                state = decay * state + sgot[zi, k].astype(F32)
            fin[k] = state

    def states_here():
        for k in Z_ORDER:
            chip_decay_got(k).wait_recv()
            state_got(k).wait_recv()

    def owner_0():
        @pl.when(x == 0)
        def _():
            st_own.wait()
            st_move.wait_recv()
            fin[...] = stin[...]
            prefix()
            t_move.start()

    def owner_1():
        @pl.when(x == 1)
        def _():
            t_move.wait_recv()
            fin[...] = t0[...]
            prefix()
            so_move.start()
            so_own.start()

    def enter_send(part):
        for k in Z_ORDER:
            go(enter_move(k, part))
        egot[z, part] = eout[z, part]

    def pair_enter(part):
        for k in Z_ORDER:
            enter_got(k, part).wait_recv()

        def step(zi, carry):
            h = 16 * part + 2 * zi + c
            entering = egot[zi, part]
            after = jnp.exp(dt[0, pl.ds(h, 1), :]) * entering.astype(F32) + s_own[2 * zi + part]
            after = after.astype(BF16)
            ent[c, part, zi] = jnp.where(first, entering, after)
            esend[part, zi] = jnp.where(first, after, entering)
            return carry

        lax.fori_loop(0, NZ, step, 0, unroll=2)
        go(enter_pair(part))

    def enter_pair(part):
        return remote(esend.at[part], ent.at[c, part], ep_s.at[part], ep_r.at[part], mate_at(1))

    def enter_pair_got(part):
        return remote(esend.at[part], ent.at[1 - c, part], ep_s.at[part], ep_r.at[part], mate_at(1))

    def carried(parity, part):
        def step(zi, carry):
            h = 16 * part + 2 * zi + parity
            reached = jnp.dot(qlv[:, block(h)], ent[parity, part, zi], preferred_element_type=F32)
            mixed = lin[:, block(h)] + jnp.exp(column(h)) * reached
            lin[:, block(h)] = mixed
            sq[...] += mixed * mixed
            return carry

        lax.fori_loop(0, NZ, step, 0, unroll=4)

    def gates():
        def step(h, carry):
            gate = 1.0 / (1.0 + jnp.exp(-gtv[:, block(h)].astype(F32)))
            gf[:, block(h)] = gain_in[:, block(h)] * gate
            return carry

        lax.fori_loop(0, LHEADS, step, 0, unroll=4)

    def gated_heads():
        mean = jnp.sum(sq[...], axis=1, keepdims=True) / (LHEADS * DH)
        factor = jnp.broadcast_to(lax.rsqrt(mean + NORM_EPS), (DH, DH))

        def gated(h, carry):
            qlv[:, block(h)] = (lin[:, block(h)] * factor * gf[:, block(h)]).astype(BF16)
            return carry

        lax.fori_loop(0, LHEADS, gated, 0, unroll=4)
        light_copy.start()

    light_copy = pltpu.make_async_copy(qlv, light_out, out_s)

    loads[3].wait()
    inner_heads(0, 16)
    pump(0, 1)
    inner_heads(16, 32)
    pump(1, 1)
    queries_here(0)
    own_slot(0)
    process(0, 1)
    queries_here(1)
    own_slot(1)
    states_here()
    owner_0()
    process(1, 1)
    pump(0, 2)
    pump(1, 2)
    owner_1()
    enter_send(0)
    process(0, 2)
    pump(0, 3)
    process(1, 2)
    pump(1, 3)
    enter_send(1)
    process(0, 3)
    loads[4].wait()
    gates()
    pump(0, 4)
    process(0, 4)
    finish_heads(0)
    process(1, 3)
    pair_enter(0)
    sq[...] = jnp.zeros_like(sq)
    carried(c, 0)
    pump(1, 4)
    process(1, 4)
    finish_heads(1)
    enter_pair_got(0).wait_recv()
    carried(1 - c, 0)
    pair_enter(1)
    carried(c, 1)
    enter_pair_got(1).wait_recv()
    carried(1 - c, 1)
    gated_heads()

    for hh in range(2):
        out_own(hh).wait()
        for p in (1, 2, 3):
            out_got(hh, p).wait_recv()
    light_copy.wait()

    @pl.when(x == 0)
    def _():
        so_move.wait_recv()
        t_move.wait_send()

    @pl.when(x == 1)
    def _():
        st_move.wait_send()
        so_own.wait()
        so_move.wait_send()

    for copy in sends:
        copy.wait_send()


def shards(*arrays):
    (query_lin, key_lin, value_lin, log_decay, out_gate, norm_gain, state_in, query_soft, key_soft,
     value_soft) = arrays
    rows, width = query_lin.shape
    hbm = pl.BlockSpec(memory_space=pl.ANY)
    vmem = pl.BlockSpec(memory_space=pltpu.VMEM)
    dma = pltpu.SemaphoreType.DMA
    state = (DH, DH)
    return pl.pallas_call(
        kernel,
        out_shape=(
            jax.ShapeDtypeStruct((rows, width), BF16),
            jax.ShapeDtypeStruct(state_in.shape, F32),
            jax.ShapeDtypeStruct((rows, width), BF16),
        ),
        in_specs=[hbm, hbm, hbm, vmem, hbm, vmem, hbm, hbm, hbm, hbm],
        out_specs=(hbm, hbm, hbm),
        scratch_shapes=[
            pltpu.VMEM((NZ, 2, 2, 2, 2 * DH, DH), BF16),
            pltpu.VMEM((2, 4, rows, 512), BF16),
            pltpu.VMEM((2, 2, 4, DH, 2 * DH), F32),
            pltpu.VMEM((2, 8, 2 * DH), F32),
            pltpu.VMEM((2, 8, 2 * DH), F32),
            pltpu.VMEM((2, 4, rows, 512), BF16),
            pltpu.VMEM((rows, 1024), BF16),
            pltpu.VMEM((8, DH, rows), BF16),
            pltpu.VMEM((rows, width), BF16),
            pltpu.VMEM((rows, width), BF16),
            pltpu.VMEM((rows, width), BF16),
            pltpu.VMEM((rows, width), BF16),
            pltpu.VMEM((rows, width), F32),
            pltpu.VMEM((LHEADS, DH), F32),
            pltpu.VMEM((DH, LHEADS), F32),
            pltpu.VMEM((16,) + state, F32),
            pltpu.VMEM((16,) + state, BF16),
            pltpu.VMEM((16,) + state, BF16),
            pltpu.VMEM((NZ, 2) + state, BF16),
            pltpu.VMEM((NZ, 2) + state, BF16),
            pltpu.VMEM((NZ, 2) + state, BF16),
            pltpu.VMEM((NZ, 2) + state, BF16),
            pltpu.VMEM((2, 2, NZ) + state, BF16),
            pltpu.VMEM((2, NZ) + state, BF16),
            pltpu.VMEM((rows, width), F32),
            pltpu.VMEM((2,) + state, F32),
            pltpu.VMEM((2,) + state, F32),
            pltpu.VMEM((2,) + state, F32),
            pltpu.VMEM((2, LHEADS, DH), F32),
            pltpu.VMEM((NZ, LHEADS, DH), F32),
            pltpu.VMEM(state, F32),
            dma((5,)),
            dma((2, 2, 4)), dma((2, 2, 4)),
            dma((2, 4)), dma((2, 4)),
            dma, dma((2,)),
            dma, dma,
            dma, dma,
            dma((7,)), dma((7,)),
            dma((7,)), dma((7,)),
            dma((2, 7)), dma((2, 7)),
            dma, dma,
            dma, dma((2,)),
            dma((2,)), dma((2,)),
            dma((2, 2, 4, 2)), dma((2, 2, 4, 2)),
            dma((2, 4)), dma((2, 4)),
            dma,
        ],
        compiler_params=pltpu.CompilerParams(
            collective_id=0, has_side_effects=True, vmem_limit_bytes=62 * 2**20
        ),
        name="window",
    )(
        query_lin, key_lin, value_lin, log_decay, out_gate, norm_gain.reshape(1, width), state_in,
        query_soft, key_soft, value_soft,
    )


def solution(mesh):
    rows = P(("dp", "seq"), None)
    states = P(("dp", "seq"), None, None)
    return jax.shard_map(
        shards,
        mesh=mesh,
        in_specs=(rows, rows, rows, rows, rows, P(), states, rows, rows, rows),
        out_specs=(rows, states, rows),
        check_vma=False,
    )
```

```python
import functools
import math

import jax
import jax.numpy as jnp
from jax import lax
from jax.experimental import pallas as pl
from jax.experimental.pallas import tpu as pltpu
from jax.sharding import PartitionSpec as P

DH = 128
NZ = 8
LHEADS = 32
NORM_EPS = 1e-6
SCALE = DH ** (-0.5)
EXP2_SCALE = SCALE * math.log2(math.e)
MASKED = -1e30
MESH = pl.DeviceIdType.MESH
F32 = jnp.float32
BF16 = jnp.bfloat16
UNROLL = 4
ROWS_BY_ROWS = (((1,), (1,)), ((), ()))
COLS_BY_COLS = (((0,), (0,)), ((), ()))
Z_ORDER = (4, 3, 5, 2, 6, 1, 7)


def place(x, z, c):
    return (x * NZ + z) * 2 + c


def block(index):
    return pl.ds(pl.multiple_of(index * DH, DH), DH)


def wide(index, width):
    return pl.ds(pl.multiple_of(index * width, width), width)


def kernel(
    ql_in, kl_in, vl_in, ld_hbm, gate_in, gain_in, state_in, q_in, k_in, v_in,
    light_out, state_out, attn_out,
    kv, qx, acc, top, low, ob, vsv, vtl,
    qlv, klv, vlv, gtv, lin, ct, cv, s_own, s_oth, s_par, ssend, sgot, eout, egot, ent, esend, gf,
    stin, t0, fin, dt, chd, sq, ld_in,
    lsem, kvs, kvr, qsend, qrecv, st_s, st_r, d_s, d_r, sp_s, sp_r, cd_s, cd_r, sa_s, sa_r,
    eo_s, eo_r, t_s, t_r, so_s, so_r, ep_s, ep_r, ag_s, ag_r, o_s, o_r, out_s,
):
    me = lax.axis_index("seq")
    x = me // (2 * NZ)
    z = (me // 2) % NZ
    c = me % 2
    quad = x * 2 + c
    mates = {1: (x, 1 - c), 2: (1 - x, c), 3: (1 - x, 1 - c)}

    def mate_quad(p):
        mx, mc = mates[p]
        return mx * 2 + mc

    def mate_at(p):
        mx, mc = mates[p]
        return place(mx, z, mc)

    def up(k):
        return (z + k) % NZ

    def remote(src, dst, send, recv, to):
        return pltpu.make_async_remote_copy(
            src_ref=src, dst_ref=dst, send_sem=send, recv_sem=recv,
            device_id={"seq": to}, device_id_type=MESH,
        )

    sends = []

    def go(copy):
        copy.start()
        sends.append(copy)

    barrier = pltpu.get_barrier_semaphore()
    peers = [mate_at(p) for p in (1, 2, 3)] + [place(x, up(k), c) for k in range(1, NZ)]
    for peer in peers:
        pl.semaphore_signal(barrier, inc=1, device_id={"seq": peer}, device_id_type=MESH)

    loads = [
        pltpu.make_async_copy(v_in, vsv, lsem.at[0]),
        pltpu.make_async_copy(kl_in, klv, lsem.at[1]),
        pltpu.make_async_copy(vl_in, vlv, lsem.at[2]),
        pltpu.make_async_copy(ql_in, qlv, lsem.at[3]),
        pltpu.make_async_copy(gate_in, gtv, lsem.at[4]),
        pltpu.make_async_copy(ld_hbm, ld_in, lsem.at[5]),
    ]
    for i in (5, 0, 1, 2, 3, 4):
        loads[i].start()
    loads[5].wait()

    def head_of(n, parity):
        return 16 * (n % 2) + 2 * (n // 2) + parity

    t_row = lax.broadcasted_iota(jnp.int32, (DH, DH), 0)
    t_col = lax.broadcasted_iota(jnp.int32, (DH, DH), 1)
    triu = jnp.where(t_row <= t_col, 1.0, 0.0).astype(BF16)
    cum_t = jnp.dot(ld_in[...], triu, preferred_element_type=F32)
    ct[...] = cum_t
    cv[...] = jnp.transpose(cum_t)
    dt[c] = jnp.broadcast_to(cum_t[:, DH - 1 :], (LHEADS, DH))

    loads[0].wait()
    for g in range(8):
        vtl[g] = jnp.transpose(vsv[:, g * DH : (g + 1) * DH])

    pl.semaphore_wait(barrier, len(peers))

    def kv_quad(hh, sel, p):
        head = mate_quad(p) * 2 + hh
        src = vtl.at[head] if sel else k_in.at[:, block(head)]
        return remote(
            src, kv.at[z, hh, x, sel, block(c), :], kvs.at[hh, sel, p], kvr.at[hh, sel, p], mate_at(p)
        )

    def kv_quad_got(hh, sel, p):
        head = mate_quad(p) * 2 + hh
        src = vtl.at[head] if sel else k_in.at[:, block(head)]
        mx, mc = mates[p]
        return remote(
            src, kv.at[z, hh, mx, sel, block(mc), :], kvs.at[hh, sel, p], kvr.at[hh, sel, p], mate_at(p)
        )

    def kv_own(hh, sel):
        head = quad * 2 + hh
        src = vtl.at[head] if sel else k_in.at[:, block(head)]
        return pltpu.make_async_copy(src, kv.at[z, hh, x, sel, block(c), :], kvr.at[hh, sel, 0])

    for hh in range(2):
        for sel in range(2):
            go(kv_quad(hh, sel, 1))
            kv_own(hh, sel).start()
    for hh in range(2):
        for p in (2, 3):
            for sel in range(2):
                go(kv_quad(hh, sel, p))
    go(remote(dt.at[c], dt.at[c], d_s, d_r, mate_at(1)))

    def ring(hh, way, step, half):
        slot = (z + (NZ - step if way == 0 else step)) % NZ
        to = place(x, up(1 if way == 0 else NZ - 1), c)
        piece = kv.at[slot, hh, x if half == 0 else 1 - x]
        return remote(piece, piece, ag_s.at[hh, way, step, half], ag_r.at[hh, way, step, half], to)

    def ring_got(hh, way, distance, half):
        slot = (z + (NZ - distance if way == 0 else distance)) % NZ
        to = place(x, up(1 if way == 0 else NZ - 1), c)
        piece = kv.at[slot, hh, x if half == 0 else 1 - x]
        step = distance - 1
        return remote(piece, piece, ag_s.at[hh, way, step, half], ag_r.at[hh, way, step, half], to)

    def reach(way, half):
        return 4 if way == half else 3

    def later(half):
        return (x == 1) if half == 0 else (x == 0)

    def goes(way, step, half):
        if way == 0:
            needed = jnp.logical_and(z >= step, z < NZ - 1)
        else:
            needed = (z + step) % NZ < reach(way, half)
        return jnp.logical_or(jnp.logical_not(later(half)), needed)

    def comes(way, distance, half):
        if way == 0:
            needed = z >= distance
        else:
            needed = (z + distance) % NZ < reach(way, half)
        return jnp.logical_or(jnp.logical_not(later(half)), needed)

    ring_sends = []

    def go_ring(hh, way, step, half):
        @pl.when(goes(way, step, half))
        def _():
            ring(hh, way, step, half).start()

        ring_sends.append((hh, way, step, half))

    def start_ring(hh, half):
        for sel in range(2):
            if half == 0:
                kv_own(hh, sel).wait()
                kv_quad_got(hh, sel, 1).wait_recv()
            else:
                kv_quad_got(hh, sel, 2).wait_recv()
                kv_quad_got(hh, sel, 3).wait_recv()
        for way in range(2):
            go_ring(hh, way, 0, half)

    def pump(hh, distance):
        for half in range(2):
            for way in range(2):
                if distance <= reach(way, half):
                    @pl.when(comes(way, distance, half))
                    def _():
                        ring_got(hh, way, distance, half).wait_recv()

                    if distance < reach(way, half):
                        go_ring(hh, way, distance, half)

    def column(h):
        lanes = lax.broadcasted_iota(jnp.int32, (DH, LHEADS), 1)
        return jnp.sum(jnp.where(lanes == h, cv[...], 0.0), axis=1, keepdims=True)

    def silu(u):
        return u / (1.0 + jnp.exp(-u))

    def block_states(parity, target):
        def step(n, carry):
            h = head_of(n, parity)
            keys = (silu(klv[:, block(h)].astype(F32)) * SCALE).astype(BF16)
            klv[:, block(h)] = keys
            col = column(h)
            decayed = (keys.astype(F32) * jnp.exp(col[DH - 1 :, :] - col)).astype(BF16)
            state = lax.dot_general(
                decayed, vlv[:, block(h)], COLS_BY_COLS, preferred_element_type=F32
            )
            target[n] = state.astype(target.dtype)
            return carry

        lax.fori_loop(0, 16, step, 0, unroll=4)

    start_ring(0, 0)
    start_ring(1, 0)
    loads[1].wait()
    loads[2].wait()
    block_states(1 - c, s_oth)
    go(remote(s_oth, s_par, sp_s, sp_r, mate_at(1)))
    start_ring(0, 1)
    block_states(c, s_own)
    start_ring(1, 1)

    def q_quad(hh, p):
        return remote(
            q_in.at[:, wide(mate_quad(p) * 2 + hh, 512)], qx.at[hh, quad],
            qsend.at[hh, p], qrecv.at[hh, p], mate_at(p),
        )

    def q_quad_got(hh, p):
        return remote(
            q_in.at[:, wide(mate_quad(p) * 2 + hh, 512)], qx.at[hh, mate_quad(p)],
            qsend.at[hh, p], qrecv.at[hh, p], mate_at(p),
        )

    def q_own(hh):
        return pltpu.make_async_copy(
            q_in.at[:, wide(quad * 2 + hh, 512)], qx.at[hh, quad], qrecv.at[hh, 0]
        )

    for hh in range(2):
        for p in (2, 3, 1):
            go(q_quad(hh, p))
        q_own(hh).start()

    st_own = pltpu.make_async_copy(state_in.at[0], stin.at[0], st_r.at[0])
    st_move = remote(state_in.at[0], stin.at[1], st_s, st_r.at[1], mate_at(2))

    @pl.when(x == 0)
    def _():
        st_own.start()

    @pl.when(x == 1)
    def _():
        st_move.start()

    remote(dt.at[c], dt.at[1 - c], d_s, d_r, mate_at(1)).wait_recv()
    remote(s_oth, s_par, sp_s, sp_r, mate_at(1)).wait_recv()
    first = c == 0
    chd[z] = dt[0] + dt[1]

    def chip_state(n, carry):
        h = head_of(n, c)
        later = jnp.exp(dt[1, pl.ds(h, 1), :])
        own, par = s_own[n], s_par[n].astype(F32)
        earlier_state = jnp.where(first, own, par)
        later_state = jnp.where(first, par, own)
        ssend[n // 2, n % 2] = (later * earlier_state + later_state).astype(BF16)
        s_own[n] = earlier_state
        return carry

    lax.fori_loop(0, 16, chip_state, 0, unroll=2)
    sgot[z] = ssend[z]

    def chip_decay(k):
        return remote(chd.at[z], chd.at[z], cd_s.at[k - 1], cd_r.at[k - 1], place(x, up(k), c))

    def chip_decay_got(k):
        slot = up(NZ - k)
        return remote(chd.at[slot], chd.at[slot], cd_s.at[k - 1], cd_r.at[k - 1], place(x, up(k), c))

    def state_move(k):
        return remote(
            ssend.at[up(k)], sgot.at[z], sa_s.at[k - 1], sa_r.at[k - 1], place(x, up(k), c)
        )

    def state_got(k):
        return remote(
            ssend.at[up(k)], sgot.at[up(NZ - k)], sa_s.at[k - 1], sa_r.at[k - 1], place(x, up(k), c)
        )

    for k in Z_ORDER:
        go(chip_decay(k))
        go(state_move(k))

    def attend(hh, half, j, slot, both, own):
        heads = pl.ds(pl.multiple_of(j * DH, DH), DH)
        queries = jnp.concatenate([qx[hh, 2 * half, :, heads], qx[hh, 2 * half + 1, :, heads]], axis=0)
        parts = (0, 1) if both else (0,)
        keys = jnp.concatenate([kv[slot, hh, i, 0] for i in parts], axis=0)
        values = jnp.concatenate(
            [kv[slot, hh, i, 1, b * DH : (b + 1) * DH, :] for i in parts for b in range(2)], axis=1
        )
        s = lax.dot_general(keys, queries, ROWS_BY_ROWS, preferred_element_type=F32)
        if own:
            count = s.shape[0]
            key = lax.broadcasted_iota(jnp.int32, s.shape, 0) - (count - 2 * DH)
            query = lax.broadcasted_iota(jnp.int32, s.shape, 1)
            s = jnp.where(key <= query, s, MASKED)
        row = pl.ds(half * 4 + j, 1)
        new = jnp.max(s, axis=0, keepdims=True)
        if not own:
            old = top[hh, row, :]
            new = jnp.maximum(old, new)
        raised = jnp.exp2((s - new) * EXP2_SCALE)
        part = jnp.sum(raised, axis=0, keepdims=True)
        summed = jnp.dot(values, raised.astype(BF16), preferred_element_type=F32)
        if own:
            low[hh, row, :] = part
            acc[hh, half, j] = summed
        else:
            fade = jnp.exp2((old - new) * EXP2_SCALE)
            low[hh, row, :] = low[hh, row, :] * fade + part
            acc[hh, half, j] = acc[hh, half, j] * fade + summed
        top[hh, row, :] = new

    def over_heads(body):
        def step(j, carry):
            body(j)
            return carry

        lax.fori_loop(0, 4, step, 0, unroll=UNROLL)

    def own_slot(hh):
        def body(j):
            attend(hh, 0, j, z, False, True)
            attend(hh, 1, j, z, True, True)

        over_heads(body)

    def other_slot(hh, slot):
        @pl.when(slot < z)
        def _():
            def body(j):
                attend(hh, 0, j, slot, False, False)
                attend(hh, 1, j, slot, True, False)

            over_heads(body)

        @pl.when(slot > z)
        def _():
            over_heads(lambda j: attend(hh, 1, j, slot, False, False))

    def process(hh, distance):
        if distance < 4:
            def step(way, carry):
                other_slot(hh, (z + NZ - distance + 2 * distance * way) % NZ)
                return carry

            lax.fori_loop(0, 2, step, 0)
        else:
            other_slot(hh, (z + distance) % NZ)

    def finish_heads(hh):
        for half in range(2):
            def step(j, carry):
                scale = 1.0 / low[hh, pl.ds(half * 4 + j, 1), :]
                result = jnp.transpose(acc[hh, half, j] * scale).astype(BF16)
                ob[hh, 2 * half, :, block(j)] = result[0:DH]
                ob[hh, 2 * half + 1, :, block(j)] = result[DH:]
                return carry

            lax.fori_loop(0, 4, step, 0, unroll=2)
        for p in (2, 3, 1):
            go(out_quad(hh, p))
        out_own(hh).start()

    def out_quad(hh, p):
        return remote(
            ob.at[hh, mate_quad(p)], attn_out.at[:, wide(quad * 2 + hh, 512)],
            o_s.at[hh, p], o_r.at[hh, p], mate_at(p),
        )

    def out_got(hh, p):
        return remote(
            ob.at[hh, mate_quad(p)], attn_out.at[:, wide(mate_quad(p) * 2 + hh, 512)],
            o_s.at[hh, p], o_r.at[hh, p], mate_at(p),
        )

    def out_own(hh):
        return pltpu.make_async_copy(
            ob.at[hh, quad], attn_out.at[:, wide(quad * 2 + hh, 512)], o_r.at[hh, 0]
        )

    def queries_here(hh):
        q_own(hh).wait()
        for p in (1, 2, 3):
            q_quad_got(hh, p).wait_recv()

    def inner_heads(begin, end):
        def step(h, carry):
            queries = silu(qlv[:, block(h)].astype(F32)).astype(BF16)
            qlv[:, block(h)] = queries
            scores = lax.dot_general(
                queries, klv[:, block(h)], ROWS_BY_ROWS, preferred_element_type=F32
            )
            spread = column(h) - ct[pl.ds(h, 1), :]
            damping = jnp.exp(jnp.where(t_row >= t_col, spread, MASKED))
            damped = (scores * damping).astype(BF16)
            lin[:, block(h)] = jnp.dot(damped, vlv[:, block(h)], preferred_element_type=F32)
            return carry

        lax.fori_loop(begin, end, step, 0, unroll=4)

    t_move = remote(fin, t0, t_s, t_r, mate_at(2))
    so_move = remote(fin.at[0], state_out.at[0], so_s, so_r.at[0], mate_at(2))
    so_own = pltpu.make_async_copy(fin.at[1], state_out.at[0], so_r.at[1])

    def enter_move(k, part):
        return remote(
            eout.at[up(k), part], egot.at[z, part],
            eo_s.at[part, k - 1], eo_r.at[part, k - 1], place(x, up(k), c),
        )

    def enter_got(k, part):
        return remote(
            eout.at[up(k), part], egot.at[up(NZ - k), part],
            eo_s.at[part, k - 1], eo_r.at[part, k - 1], place(x, up(k), c),
        )

    def prefix():
        for k in range(2):
            state = fin[k]
            for zi in range(NZ):
                eout[zi, k] = state.astype(BF16)
                decay = jnp.exp(chd[zi, pl.ds(16 * k + 2 * z + c, 1), :])
                state = decay * state + sgot[zi, k].astype(F32)
            fin[k] = state

    def states_here():
        for k in Z_ORDER:
            chip_decay_got(k).wait_recv()
            state_got(k).wait_recv()

    def owner_0():
        @pl.when(x == 0)
        def _():
            st_own.wait()
            st_move.wait_recv()
            fin[...] = stin[...]
            prefix()
            t_move.start()

    def owner_1():
        @pl.when(x == 1)
        def _():
            t_move.wait_recv()
            fin[...] = t0[...]
            prefix()
            so_move.start()
            so_own.start()

    def enter_send(part):
        for k in Z_ORDER:
            go(enter_move(k, part))
        egot[z, part] = eout[z, part]

    def pair_enter(part):
        for k in Z_ORDER:
            enter_got(k, part).wait_recv()

        def step(zi, carry):
            h = 16 * part + 2 * zi + c
            entering = egot[zi, part]
            after = jnp.exp(dt[0, pl.ds(h, 1), :]) * entering.astype(F32) + s_own[2 * zi + part]
            after = after.astype(BF16)
            ent[c, part, zi] = jnp.where(first, entering, after)
            esend[part, zi] = jnp.where(first, after, entering)
            return carry

        lax.fori_loop(0, NZ, step, 0, unroll=2)
        go(enter_pair(part))

    def enter_pair(part):
        return remote(esend.at[part], ent.at[c, part], ep_s.at[part], ep_r.at[part], mate_at(1))

    def enter_pair_got(part):
        return remote(esend.at[part], ent.at[1 - c, part], ep_s.at[part], ep_r.at[part], mate_at(1))

    def carried(parity, part):
        def step(zi, carry):
            h = 16 * part + 2 * zi + parity
            reached = jnp.dot(qlv[:, block(h)], ent[parity, part, zi], preferred_element_type=F32)
            mixed = lin[:, block(h)] + jnp.exp(column(h)) * reached
            lin[:, block(h)] = mixed
            sq[...] += mixed * mixed
            return carry

        lax.fori_loop(0, NZ, step, 0, unroll=4)

    def gates():
        def step(h, carry):
            gate = 1.0 / (1.0 + jnp.exp(-gtv[:, block(h)].astype(F32)))
            gf[:, block(h)] = gain_in[:, block(h)] * gate
            return carry

        lax.fori_loop(0, LHEADS, step, 0, unroll=4)

    def gated_heads():
        mean = jnp.sum(sq[...], axis=1, keepdims=True) / (LHEADS * DH)
        factor = jnp.broadcast_to(lax.rsqrt(mean + NORM_EPS), (DH, DH))

        def gated(h, carry):
            qlv[:, block(h)] = (lin[:, block(h)] * factor * gf[:, block(h)]).astype(BF16)
            return carry

        lax.fori_loop(0, LHEADS, gated, 0, unroll=4)
        light_copy.start()

    light_copy = pltpu.make_async_copy(qlv, light_out, out_s)

    loads[3].wait()
    inner_heads(0, 16)
    pump(0, 1)
    inner_heads(16, 32)
    pump(1, 1)
    queries_here(0)
    own_slot(0)
    process(0, 1)
    queries_here(1)
    own_slot(1)
    states_here()
    owner_0()
    process(1, 1)
    pump(0, 2)
    pump(1, 2)
    owner_1()
    process(0, 2)
    pump(0, 3)
    enter_send(0)
    process(1, 2)
    pump(1, 3)
    enter_send(1)
    process(0, 3)
    loads[4].wait()
    gates()
    pump(0, 4)
    process(0, 4)
    finish_heads(0)
    process(1, 3)
    pair_enter(0)
    sq[...] = jnp.zeros_like(sq)
    carried(c, 0)
    pump(1, 4)
    process(1, 4)
    finish_heads(1)
    enter_pair_got(0).wait_recv()
    carried(1 - c, 0)
    pair_enter(1)
    carried(c, 1)
    enter_pair_got(1).wait_recv()
    carried(1 - c, 1)
    gated_heads()

    for hh in range(2):
        out_own(hh).wait()
        for p in (1, 2, 3):
            out_got(hh, p).wait_recv()
    light_copy.wait()

    @pl.when(x == 0)
    def _():
        so_move.wait_recv()
        t_move.wait_send()

    @pl.when(x == 1)
    def _():
        st_move.wait_send()
        so_own.wait()
        so_move.wait_send()

    for copy in sends:
        copy.wait_send()
    for hh, way, step, half in ring_sends:
        @pl.when(goes(way, step, half))
        def _():
            ring(hh, way, step, half).wait_send()


def hand_over(light_in, state_in, attn_in, light_out, state_out, attn_out, light, state, attn, sem):
    rows = light.shape[0] // 4
    moves = [(state_in, state, state_out)]
    for i in range(4):
        part = pl.ds(i * rows, rows)
        moves.append((light_in.at[part, :], light.at[part, :], light_out.at[part, :]))
        moves.append((attn_in.at[part, :], attn.at[part, :], attn_out.at[part, :]))
    into = [pltpu.make_async_copy(a, b, sem.at[0, i]) for i, (a, b, _) in enumerate(moves)]
    out = [pltpu.make_async_copy(b, a, sem.at[1, i]) for i, (_, b, a) in enumerate(moves)]
    for copy in into:
        copy.start()
    for i in range(len(moves)):
        into[i].wait()
        out[i].start()
    for copy in out:
        copy.wait()


def shards(*arrays):
    (query_lin, key_lin, value_lin, log_decay, out_gate, norm_gain, state_in, query_soft, key_soft,
     value_soft) = arrays
    rows, width = query_lin.shape
    hbm = pl.BlockSpec(memory_space=pl.ANY)
    vmem = pl.BlockSpec(memory_space=pltpu.VMEM)
    dma = pltpu.SemaphoreType.DMA
    state = (DH, DH)
    shapes = (
        jax.ShapeDtypeStruct((rows, width), BF16),
        jax.ShapeDtypeStruct(state_in.shape, F32),
        jax.ShapeDtypeStruct((rows, width), BF16),
    )
    results = pl.pallas_call(
        kernel,
        out_shape=shapes,
        in_specs=[hbm, hbm, hbm, hbm, hbm, vmem, hbm, hbm, hbm, hbm],
        out_specs=(hbm, hbm, hbm),
        scratch_shapes=[
            pltpu.VMEM((NZ, 2, 2, 2, 2 * DH, DH), BF16),
            pltpu.VMEM((2, 4, rows, 512), BF16),
            pltpu.VMEM((2, 2, 4, DH, 2 * DH), F32),
            pltpu.VMEM((2, 8, 2 * DH), F32),
            pltpu.VMEM((2, 8, 2 * DH), F32),
            pltpu.VMEM((2, 4, rows, 512), BF16),
            pltpu.VMEM((rows, 1024), BF16),
            pltpu.VMEM((8, DH, rows), BF16),
            pltpu.VMEM((rows, width), BF16),
            pltpu.VMEM((rows, width), BF16),
            pltpu.VMEM((rows, width), BF16),
            pltpu.VMEM((rows, width), BF16),
            pltpu.VMEM((rows, width), F32),
            pltpu.VMEM((LHEADS, DH), F32),
            pltpu.VMEM((DH, LHEADS), F32),
            pltpu.VMEM((16,) + state, F32),
            pltpu.VMEM((16,) + state, BF16),
            pltpu.VMEM((16,) + state, BF16),
            pltpu.VMEM((NZ, 2) + state, BF16),
            pltpu.VMEM((NZ, 2) + state, BF16),
            pltpu.VMEM((NZ, 2) + state, BF16),
            pltpu.VMEM((NZ, 2) + state, BF16),
            pltpu.VMEM((2, 2, NZ) + state, BF16),
            pltpu.VMEM((2, NZ) + state, BF16),
            pltpu.VMEM((rows, width), F32),
            pltpu.VMEM((2,) + state, F32),
            pltpu.VMEM((2,) + state, F32),
            pltpu.VMEM((2,) + state, F32),
            pltpu.VMEM((2, LHEADS, DH), F32),
            pltpu.VMEM((NZ, LHEADS, DH), F32),
            pltpu.VMEM(state, F32),
            pltpu.VMEM((LHEADS, rows), BF16),
            dma((6,)),
            dma((2, 2, 4)), dma((2, 2, 4)),
            dma((2, 4)), dma((2, 4)),
            dma, dma((2,)),
            dma, dma,
            dma, dma,
            dma((7,)), dma((7,)),
            dma((7,)), dma((7,)),
            dma((2, 7)), dma((2, 7)),
            dma, dma,
            dma, dma((2,)),
            dma((2,)), dma((2,)),
            dma((2, 2, 4, 2)), dma((2, 2, 4, 2)),
            dma((2, 4)), dma((2, 4)),
            dma,
        ],
        compiler_params=pltpu.CompilerParams(
            collective_id=0, has_side_effects=True, vmem_limit_bytes=62 * 2**20
        ),
        name="window",
    )(
        query_lin, key_lin, value_lin, log_decay.T, out_gate, norm_gain.reshape(1, width), state_in,
        query_soft, key_soft, value_soft,
    )
    return pl.pallas_call(
        hand_over,
        out_shape=shapes,
        in_specs=[hbm, hbm, hbm],
        out_specs=(hbm, hbm, hbm),
        scratch_shapes=[
            pltpu.VMEM((rows, width), BF16),
            pltpu.VMEM(state_in.shape, F32),
            pltpu.VMEM((rows, width), BF16),
            dma((2, 9)),
        ],
        compiler_params=pltpu.CompilerParams(vmem_limit_bytes=62 * 2**20),
        name="hand_over",
    )(*results)


def solution(mesh):
    rows = P(("dp", "seq"), None)
    states = P(("dp", "seq"), None, None)
    return jax.shard_map(
        shards,
        mesh=mesh,
        in_specs=(rows, rows, rows, rows, rows, P(), states, rows, rows, rows),
        out_specs=(rows, states, rows),
        check_vma=False,
    )
```

```python
import functools
import math

import jax
import jax.numpy as jnp
from jax import lax
from jax.experimental import pallas as pl
from jax.experimental.pallas import tpu as pltpu
from jax.sharding import PartitionSpec as P

DH = 128
NZ = 8
LHEADS = 32
NORM_EPS = 1e-6
SCALE = DH ** (-0.5)
EXP2_SCALE = SCALE * math.log2(math.e)
MASKED = -1e30
MESH = pl.DeviceIdType.MESH
F32 = jnp.float32
BF16 = jnp.bfloat16
UNROLL = 4
ROWS_BY_ROWS = (((1,), (1,)), ((), ()))
COLS_BY_COLS = (((0,), (0,)), ((), ()))
Z_ORDER = (4, 3, 5, 2, 6, 1, 7)


def place(x, z, c):
    return (x * NZ + z) * 2 + c


def block(index):
    return pl.ds(pl.multiple_of(index * DH, DH), DH)


def wide(index, width):
    return pl.ds(pl.multiple_of(index * width, width), width)


def kernel(
    ql_in, kl_in, vl_in, ld_hbm, gate_in, gain_in, state_in, q_in, k_in, v_in,
    light_out, state_out, attn_out,
    kv, qx, acc, top, low, ob, vsv, vtl,
    qlv, klv, vlv, gtv, lin, ct, cv, s_own, s_oth, s_par, ssend, sgot, eout, egot, ent, esend, gf,
    stin, t0, fin, dt, chd, sq, ld_in,
    lsem, kvs, kvr, qsend, qrecv, st_s, st_r, d_s, d_r, sp_s, sp_r, cd_s, cd_r, sa_s, sa_r,
    eo_s, eo_r, t_s, t_r, so_s, so_r, ep_s, ep_r, ag_s, ag_r, o_s, o_r, out_s,
):
    me = lax.axis_index("seq")
    x = me // (2 * NZ)
    z = (me // 2) % NZ
    c = me % 2
    quad = x * 2 + c
    mates = {1: (x, 1 - c), 2: (1 - x, c), 3: (1 - x, 1 - c)}

    def mate_quad(p):
        mx, mc = mates[p]
        return mx * 2 + mc

    def mate_at(p):
        mx, mc = mates[p]
        return place(mx, z, mc)

    def up(k):
        return (z + k) % NZ

    def remote(src, dst, send, recv, to):
        return pltpu.make_async_remote_copy(
            src_ref=src, dst_ref=dst, send_sem=send, recv_sem=recv,
            device_id={"seq": to}, device_id_type=MESH,
        )

    sends = []

    def go(copy):
        copy.start()
        sends.append(copy)

    barrier = pltpu.get_barrier_semaphore()
    peers = [mate_at(p) for p in (1, 2, 3)] + [place(x, up(k), c) for k in range(1, NZ)]
    for peer in peers:
        pl.semaphore_signal(barrier, inc=1, device_id={"seq": peer}, device_id_type=MESH)

    loads = [
        pltpu.make_async_copy(v_in, vsv, lsem.at[0]),
        pltpu.make_async_copy(kl_in, klv, lsem.at[1]),
        pltpu.make_async_copy(vl_in, vlv, lsem.at[2]),
        pltpu.make_async_copy(ql_in, qlv, lsem.at[3]),
        pltpu.make_async_copy(gate_in, gtv, lsem.at[4]),
        pltpu.make_async_copy(ld_hbm, ld_in, lsem.at[5]),
    ]
    for i in (5, 0, 1, 2, 3, 4):
        loads[i].start()
    loads[5].wait()

    def head_of(n, parity):
        return 16 * (n % 2) + 2 * (n // 2) + parity

    t_row = lax.broadcasted_iota(jnp.int32, (DH, DH), 0)
    t_col = lax.broadcasted_iota(jnp.int32, (DH, DH), 1)
    triu = jnp.where(t_row <= t_col, 1.0, 0.0).astype(BF16)
    cum_t = jnp.dot(ld_in[...], triu, preferred_element_type=F32)
    ct[...] = cum_t
    cv[...] = jnp.transpose(cum_t)
    dt[c] = jnp.broadcast_to(cum_t[:, DH - 1 :], (LHEADS, DH))

    loads[0].wait()
    for g in range(8):
        vtl[g] = jnp.transpose(vsv[:, g * DH : (g + 1) * DH])

    pl.semaphore_wait(barrier, len(peers))

    def kv_quad(hh, sel, p):
        head = mate_quad(p) * 2 + hh
        src = vtl.at[head] if sel else k_in.at[:, block(head)]
        return remote(
            src, kv.at[z, hh, x, sel, block(c), :], kvs.at[hh, sel, p], kvr.at[hh, sel, p], mate_at(p)
        )

    def kv_quad_got(hh, sel, p):
        head = mate_quad(p) * 2 + hh
        src = vtl.at[head] if sel else k_in.at[:, block(head)]
        mx, mc = mates[p]
        return remote(
            src, kv.at[z, hh, mx, sel, block(mc), :], kvs.at[hh, sel, p], kvr.at[hh, sel, p], mate_at(p)
        )

    def kv_own(hh, sel):
        head = quad * 2 + hh
        src = vtl.at[head] if sel else k_in.at[:, block(head)]
        return pltpu.make_async_copy(src, kv.at[z, hh, x, sel, block(c), :], kvr.at[hh, sel, 0])

    for hh in range(2):
        for sel in range(2):
            go(kv_quad(hh, sel, 1))
            kv_own(hh, sel).start()
    for hh in range(2):
        for p in (2, 3):
            for sel in range(2):
                go(kv_quad(hh, sel, p))
    go(remote(dt.at[c], dt.at[c], d_s, d_r, mate_at(1)))

    def ring(hh, way, step, half):
        slot = (z + (NZ - step if way == 0 else step)) % NZ
        to = place(x, up(1 if way == 0 else NZ - 1), c)
        piece = kv.at[slot, hh, x if half == 0 else 1 - x]
        return remote(piece, piece, ag_s.at[hh, way, step, half], ag_r.at[hh, way, step, half], to)

    def ring_got(hh, way, distance, half):
        slot = (z + (NZ - distance if way == 0 else distance)) % NZ
        to = place(x, up(1 if way == 0 else NZ - 1), c)
        piece = kv.at[slot, hh, x if half == 0 else 1 - x]
        step = distance - 1
        return remote(piece, piece, ag_s.at[hh, way, step, half], ag_r.at[hh, way, step, half], to)

    def reach(way, half):
        return 4 if way == half else 3

    def later(half):
        return (x == 1) if half == 0 else (x == 0)

    def goes(way, step, half):
        if way == 0:
            needed = jnp.logical_and(z >= step, z < NZ - 1)
        else:
            needed = (z + step) % NZ < reach(way, half)
        return jnp.logical_or(jnp.logical_not(later(half)), needed)

    def comes(way, distance, half):
        if way == 0:
            needed = z >= distance
        else:
            needed = (z + distance) % NZ < reach(way, half)
        return jnp.logical_or(jnp.logical_not(later(half)), needed)

    ring_sends = []

    def go_ring(hh, way, step, half):
        @pl.when(goes(way, step, half))
        def _():
            ring(hh, way, step, half).start()

        ring_sends.append((hh, way, step, half))

    def start_ring(hh, half):
        for sel in range(2):
            if half == 0:
                kv_own(hh, sel).wait()
                kv_quad_got(hh, sel, 1).wait_recv()
            else:
                kv_quad_got(hh, sel, 2).wait_recv()
                kv_quad_got(hh, sel, 3).wait_recv()
        for way in range(2):
            go_ring(hh, way, 0, half)

    def pump(hh, distance):
        for half in range(2):
            for way in range(2):
                if distance <= reach(way, half):
                    @pl.when(comes(way, distance, half))
                    def _():
                        ring_got(hh, way, distance, half).wait_recv()

                    if distance < reach(way, half):
                        go_ring(hh, way, distance, half)

    def column(h):
        lanes = lax.broadcasted_iota(jnp.int32, (DH, LHEADS), 1)
        return jnp.sum(jnp.where(lanes == h, cv[...], 0.0), axis=1, keepdims=True)

    def silu(u):
        return u / (1.0 + jnp.exp(-u))

    def block_states(parity, target):
        def step(n, carry):
            h = head_of(n, parity)
            keys = (silu(klv[:, block(h)].astype(F32)) * SCALE).astype(BF16)
            klv[:, block(h)] = keys
            col = column(h)
            decayed = (keys.astype(F32) * jnp.exp(col[DH - 1 :, :] - col)).astype(BF16)
            state = lax.dot_general(
                decayed, vlv[:, block(h)], COLS_BY_COLS, preferred_element_type=F32
            )
            target[n] = state.astype(target.dtype)
            return carry

        lax.fori_loop(0, 16, step, 0, unroll=4)

    start_ring(0, 0)
    start_ring(1, 0)
    loads[1].wait()
    loads[2].wait()
    block_states(1 - c, s_oth)
    go(remote(s_oth, s_par, sp_s, sp_r, mate_at(1)))
    start_ring(0, 1)
    block_states(c, s_own)
    start_ring(1, 1)

    def q_quad(hh, p):
        return remote(
            q_in.at[:, wide(mate_quad(p) * 2 + hh, 512)], qx.at[hh, quad],
            qsend.at[hh, p], qrecv.at[hh, p], mate_at(p),
        )

    def q_quad_got(hh, p):
        return remote(
            q_in.at[:, wide(mate_quad(p) * 2 + hh, 512)], qx.at[hh, mate_quad(p)],
            qsend.at[hh, p], qrecv.at[hh, p], mate_at(p),
        )

    def q_own(hh):
        return pltpu.make_async_copy(
            q_in.at[:, wide(quad * 2 + hh, 512)], qx.at[hh, quad], qrecv.at[hh, 0]
        )

    for hh in range(2):
        for p in (2, 3, 1):
            go(q_quad(hh, p))
        q_own(hh).start()

    st_own = pltpu.make_async_copy(state_in.at[0], stin.at[0], st_r.at[0])
    st_move = remote(state_in.at[0], stin.at[1], st_s, st_r.at[1], mate_at(2))

    @pl.when(x == 0)
    def _():
        st_own.start()

    @pl.when(x == 1)
    def _():
        st_move.start()

    remote(dt.at[c], dt.at[1 - c], d_s, d_r, mate_at(1)).wait_recv()
    remote(s_oth, s_par, sp_s, sp_r, mate_at(1)).wait_recv()
    first = c == 0
    chd[z] = jnp.transpose(dt[0] + dt[1])[0:8, :]

    def chip_state(n, carry):
        h = head_of(n, c)
        later = jnp.exp(dt[1, pl.ds(h, 1), :])
        own, par = s_own[n], s_par[n].astype(F32)
        earlier_state = jnp.where(first, own, par)
        later_state = jnp.where(first, par, own)
        ssend[n // 2, n % 2] = (later * earlier_state + later_state).astype(BF16)
        s_own[n] = earlier_state
        return carry

    lax.fori_loop(0, 16, chip_state, 0, unroll=2)
    sgot[z] = ssend[z]

    def chip_decay(k):
        return remote(chd.at[z], chd.at[z], cd_s.at[k - 1], cd_r.at[k - 1], place(x, up(k), c))

    def chip_decay_got(k):
        slot = up(NZ - k)
        return remote(chd.at[slot], chd.at[slot], cd_s.at[k - 1], cd_r.at[k - 1], place(x, up(k), c))

    def state_move(k):
        return remote(
            ssend.at[up(k)], sgot.at[z], sa_s.at[k - 1], sa_r.at[k - 1], place(x, up(k), c)
        )

    def state_got(k):
        return remote(
            ssend.at[up(k)], sgot.at[up(NZ - k)], sa_s.at[k - 1], sa_r.at[k - 1], place(x, up(k), c)
        )

    for k in Z_ORDER:
        go(chip_decay(k))
        go(state_move(k))

    def attend(hh, half, j, slot, both, own):
        heads = pl.ds(pl.multiple_of(j * DH, DH), DH)
        queries = jnp.concatenate([qx[hh, 2 * half, :, heads], qx[hh, 2 * half + 1, :, heads]], axis=0)
        parts = (0, 1) if both else (0,)
        row = pl.ds(half * 4 + j, 1)
        scores = [
            lax.dot_general(kv[slot, hh, i, 0], queries, ROWS_BY_ROWS, preferred_element_type=F32)
            for i in parts
        ]
        if own:
            key = lax.broadcasted_iota(jnp.int32, (2 * DH, 2 * DH), 0)
            query = lax.broadcasted_iota(jnp.int32, (2 * DH, 2 * DH), 1)
            scores[-1] = jnp.where(key <= query, scores[-1], MASKED)
        new = functools.reduce(jnp.maximum, [jnp.max(s, axis=0, keepdims=True) for s in scores])
        if not own:
            old = top[hh, row, :]
            new = jnp.maximum(old, new)
        part, summed = None, None
        for i, s in zip(parts, scores):
            raised = jnp.exp2((s - new) * EXP2_SCALE)
            values = jnp.concatenate([kv[slot, hh, i, 1, :DH, :], kv[slot, hh, i, 1, DH:, :]], axis=1)
            more = jnp.sum(raised, axis=0, keepdims=True)
            product = jnp.dot(values, raised.astype(BF16), preferred_element_type=F32)
            part = more if part is None else part + more
            summed = product if summed is None else summed + product
        if own:
            low[hh, row, :] = part
            acc[hh, half, j] = summed
        else:
            fade = jnp.exp2((old - new) * EXP2_SCALE)
            low[hh, row, :] = low[hh, row, :] * fade + part
            acc[hh, half, j] = acc[hh, half, j] * fade + summed
        top[hh, row, :] = new

    def over_heads(body):
        def step(j, carry):
            body(j)
            return carry

        lax.fori_loop(0, 4, step, 0, unroll=UNROLL)

    def own_slot(hh):
        def body(j):
            attend(hh, 0, j, z, False, True)
            attend(hh, 1, j, z, True, True)

        over_heads(body)

    def other_slot(hh, slot):
        @pl.when(slot < z)
        def _():
            def body(j):
                attend(hh, 0, j, slot, False, False)
                attend(hh, 1, j, slot, True, False)

            over_heads(body)

        @pl.when(slot > z)
        def _():
            over_heads(lambda j: attend(hh, 1, j, slot, False, False))

    def process(hh, distance):
        if distance < 4:
            def step(way, carry):
                other_slot(hh, (z + NZ - distance + 2 * distance * way) % NZ)
                return carry

            lax.fori_loop(0, 2, step, 0)
        else:
            other_slot(hh, (z + distance) % NZ)

    def finish_heads(hh):
        for half in range(2):
            def step(j, carry):
                scale = 1.0 / low[hh, pl.ds(half * 4 + j, 1), :]
                result = jnp.transpose(acc[hh, half, j] * scale).astype(BF16)
                ob[hh, 2 * half, :, block(j)] = result[0:DH]
                ob[hh, 2 * half + 1, :, block(j)] = result[DH:]
                return carry

            lax.fori_loop(0, 4, step, 0, unroll=2)
        for p in (2, 3, 1):
            go(out_quad(hh, p))
        out_own(hh).start()

    def out_quad(hh, p):
        return remote(
            ob.at[hh, mate_quad(p)], attn_out.at[:, wide(quad * 2 + hh, 512)],
            o_s.at[hh, p], o_r.at[hh, p], mate_at(p),
        )

    def out_got(hh, p):
        return remote(
            ob.at[hh, mate_quad(p)], attn_out.at[:, wide(mate_quad(p) * 2 + hh, 512)],
            o_s.at[hh, p], o_r.at[hh, p], mate_at(p),
        )

    def out_own(hh):
        return pltpu.make_async_copy(
            ob.at[hh, quad], attn_out.at[:, wide(quad * 2 + hh, 512)], o_r.at[hh, 0]
        )

    def queries_here(hh):
        q_own(hh).wait()
        for p in (1, 2, 3):
            q_quad_got(hh, p).wait_recv()

    def inner_heads(begin, end):
        def step(h, carry):
            queries = silu(qlv[:, block(h)].astype(F32)).astype(BF16)
            qlv[:, block(h)] = queries
            scores = lax.dot_general(
                queries, klv[:, block(h)], ROWS_BY_ROWS, preferred_element_type=F32
            )
            spread = column(h) - ct[pl.ds(h, 1), :]
            damping = jnp.exp(jnp.where(t_row >= t_col, spread, MASKED))
            damped = (scores * damping).astype(BF16)
            lin[:, block(h)] = jnp.dot(damped, vlv[:, block(h)], preferred_element_type=F32)
            return carry

        lax.fori_loop(begin, end, step, 0, unroll=4)

    t_move = remote(fin, t0, t_s, t_r, mate_at(2))
    so_move = remote(fin.at[0], state_out.at[0], so_s, so_r.at[0], mate_at(2))
    so_own = pltpu.make_async_copy(fin.at[1], state_out.at[0], so_r.at[1])

    def enter_move(k, part):
        return remote(
            eout.at[up(k), part], egot.at[z, part],
            eo_s.at[part, k - 1], eo_r.at[part, k - 1], place(x, up(k), c),
        )

    def enter_got(k, part):
        return remote(
            eout.at[up(k), part], egot.at[up(NZ - k), part],
            eo_s.at[part, k - 1], eo_r.at[part, k - 1], place(x, up(k), c),
        )

    def prefix():
        lanes = lax.broadcasted_iota(jnp.int32, (8, LHEADS), 1)
        for k in range(2):
            state = fin[k]
            for zi in range(NZ):
                eout[zi, k] = state.astype(BF16)
                total = jnp.where(lanes == 16 * k + 2 * z + c, chd[zi], 0.0)
                decay = jnp.exp(jnp.sum(total, axis=1, keepdims=True))[0:1, :]
                state = decay * state + sgot[zi, k].astype(F32)
            fin[k] = state

    def states_here():
        for k in Z_ORDER:
            chip_decay_got(k).wait_recv()
            state_got(k).wait_recv()

    def owner_0():
        @pl.when(x == 0)
        def _():
            st_own.wait()
            st_move.wait_recv()
            fin[...] = stin[...]
            prefix()
            t_move.start()

    def owner_1():
        @pl.when(x == 1)
        def _():
            t_move.wait_recv()
            fin[...] = t0[...]
            prefix()
            so_move.start()
            so_own.start()

    def enter_send(part):
        for k in Z_ORDER:
            go(enter_move(k, part))
        egot[z, part] = eout[z, part]

    def pair_enter(part):
        for k in Z_ORDER:
            enter_got(k, part).wait_recv()

        def step(zi, carry):
            h = 16 * part + 2 * zi + c
            entering = egot[zi, part]
            after = jnp.exp(dt[0, pl.ds(h, 1), :]) * entering.astype(F32) + s_own[2 * zi + part]
            after = after.astype(BF16)
            ent[c, part, zi] = jnp.where(first, entering, after)
            esend[part, zi] = jnp.where(first, after, entering)
            return carry

        lax.fori_loop(0, NZ, step, 0, unroll=2)
        go(enter_pair(part))

    def enter_pair(part):
        return remote(esend.at[part], ent.at[c, part], ep_s.at[part], ep_r.at[part], mate_at(1))

    def enter_pair_got(part):
        return remote(esend.at[part], ent.at[1 - c, part], ep_s.at[part], ep_r.at[part], mate_at(1))

    def carried(parity, part):
        def step(zi, carry):
            h = 16 * part + 2 * zi + parity
            reached = jnp.dot(qlv[:, block(h)], ent[parity, part, zi], preferred_element_type=F32)
            mixed = lin[:, block(h)] + jnp.exp(column(h)) * reached
            lin[:, block(h)] = mixed
            sq[...] += mixed * mixed
            return carry

        lax.fori_loop(0, NZ, step, 0, unroll=4)

    def gates():
        def step(h, carry):
            gate = 1.0 / (1.0 + jnp.exp(-gtv[:, block(h)].astype(F32)))
            gf[:, block(h)] = gain_in[:, block(h)] * gate
            return carry

        lax.fori_loop(0, LHEADS, step, 0, unroll=4)

    def gated_heads():
        mean = jnp.sum(sq[...], axis=1, keepdims=True) / (LHEADS * DH)
        factor = jnp.broadcast_to(lax.rsqrt(mean + NORM_EPS), (DH, DH))

        def gated(h, carry):
            qlv[:, block(h)] = (lin[:, block(h)] * factor * gf[:, block(h)]).astype(BF16)
            return carry

        lax.fori_loop(0, LHEADS, gated, 0, unroll=4)
        light_copy.start()

    light_copy = pltpu.make_async_copy(qlv, light_out, out_s)

    loads[3].wait()
    inner_heads(0, 16)
    pump(0, 1)
    inner_heads(16, 32)
    pump(1, 1)
    loads[4].wait()
    gates()
    queries_here(0)
    own_slot(0)
    process(0, 1)
    queries_here(1)
    pump(0, 2)
    own_slot(1)
    states_here()
    owner_0()
    pump(1, 2)
    process(1, 1)
    owner_1()
    pump(0, 3)
    enter_send(0)
    process(0, 2)
    process(1, 2)
    pump(1, 3)
    enter_send(1)
    process(0, 3)
    pump(0, 4)
    process(0, 4)
    finish_heads(0)
    process(1, 3)
    pair_enter(0)
    sq[...] = jnp.zeros_like(sq)
    carried(c, 0)
    pump(1, 4)
    process(1, 4)
    finish_heads(1)
    enter_pair_got(0).wait_recv()
    carried(1 - c, 0)
    pair_enter(1)
    carried(c, 1)
    enter_pair_got(1).wait_recv()
    carried(1 - c, 1)
    gated_heads()

    for hh in range(2):
        out_own(hh).wait()
        for p in (1, 2, 3):
            out_got(hh, p).wait_recv()
    light_copy.wait()

    @pl.when(x == 0)
    def _():
        so_move.wait_recv()
        t_move.wait_send()

    @pl.when(x == 1)
    def _():
        st_move.wait_send()
        so_own.wait()
        so_move.wait_send()

    for copy in sends:
        copy.wait_send()
    for hh, way, step, half in ring_sends:
        @pl.when(goes(way, step, half))
        def _():
            ring(hh, way, step, half).wait_send()


def hand_over(light_in, state_in, attn_in, light_out, state_out, attn_out, light, state, attn, sem):
    rows = light.shape[0] // 4
    moves = [(state_in, state, state_out)]
    for i in range(4):
        part = pl.ds(i * rows, rows)
        moves.append((light_in.at[part, :], light.at[part, :], light_out.at[part, :]))
        moves.append((attn_in.at[part, :], attn.at[part, :], attn_out.at[part, :]))
    into = [pltpu.make_async_copy(a, b, sem.at[0, i]) for i, (a, b, _) in enumerate(moves)]
    out = [pltpu.make_async_copy(b, a, sem.at[1, i]) for i, (_, b, a) in enumerate(moves)]
    for copy in into:
        copy.start()
    for i in range(len(moves)):
        into[i].wait()
        out[i].start()
    for copy in out:
        copy.wait()


def shards(*arrays):
    (query_lin, key_lin, value_lin, log_decay, out_gate, norm_gain, state_in, query_soft, key_soft,
     value_soft) = arrays
    rows, width = query_lin.shape
    hbm = pl.BlockSpec(memory_space=pl.ANY)
    vmem = pl.BlockSpec(memory_space=pltpu.VMEM)
    dma = pltpu.SemaphoreType.DMA
    state = (DH, DH)
    shapes = (
        jax.ShapeDtypeStruct((rows, width), BF16),
        jax.ShapeDtypeStruct(state_in.shape, F32),
        jax.ShapeDtypeStruct((rows, width), BF16),
    )
    results = pl.pallas_call(
        kernel,
        out_shape=shapes,
        in_specs=[hbm, hbm, hbm, hbm, hbm, vmem, hbm, hbm, hbm, hbm],
        out_specs=(hbm, hbm, hbm),
        scratch_shapes=[
            pltpu.VMEM((NZ, 2, 2, 2, 2 * DH, DH), BF16),
            pltpu.VMEM((2, 4, rows, 512), BF16),
            pltpu.VMEM((2, 2, 4, DH, 2 * DH), F32),
            pltpu.VMEM((2, 8, 2 * DH), F32),
            pltpu.VMEM((2, 8, 2 * DH), F32),
            pltpu.VMEM((2, 4, rows, 512), BF16),
            pltpu.VMEM((rows, 1024), BF16),
            pltpu.VMEM((8, DH, rows), BF16),
            pltpu.VMEM((rows, width), BF16),
            pltpu.VMEM((rows, width), BF16),
            pltpu.VMEM((rows, width), BF16),
            pltpu.VMEM((rows, width), BF16),
            pltpu.VMEM((rows, width), F32),
            pltpu.VMEM((LHEADS, DH), F32),
            pltpu.VMEM((DH, LHEADS), F32),
            pltpu.VMEM((16,) + state, F32),
            pltpu.VMEM((16,) + state, BF16),
            pltpu.VMEM((16,) + state, BF16),
            pltpu.VMEM((NZ, 2) + state, BF16),
            pltpu.VMEM((NZ, 2) + state, BF16),
            pltpu.VMEM((NZ, 2) + state, BF16),
            pltpu.VMEM((NZ, 2) + state, BF16),
            pltpu.VMEM((2, 2, NZ) + state, BF16),
            pltpu.VMEM((2, NZ) + state, BF16),
            pltpu.VMEM((rows, width), F32),
            pltpu.VMEM((2,) + state, F32),
            pltpu.VMEM((2,) + state, F32),
            pltpu.VMEM((2,) + state, F32),
            pltpu.VMEM((2, LHEADS, DH), F32),
            pltpu.VMEM((NZ, 8, LHEADS), F32),
            pltpu.VMEM(state, F32),
            pltpu.VMEM((LHEADS, rows), BF16),
            dma((6,)),
            dma((2, 2, 4)), dma((2, 2, 4)),
            dma((2, 4)), dma((2, 4)),
            dma, dma((2,)),
            dma, dma,
            dma, dma,
            dma((7,)), dma((7,)),
            dma((7,)), dma((7,)),
            dma((2, 7)), dma((2, 7)),
            dma, dma,
            dma, dma((2,)),
            dma((2,)), dma((2,)),
            dma((2, 2, 4, 2)), dma((2, 2, 4, 2)),
            dma((2, 4)), dma((2, 4)),
            dma,
        ],
        compiler_params=pltpu.CompilerParams(
            collective_id=0, has_side_effects=True, vmem_limit_bytes=62 * 2**20
        ),
        name="window",
    )(
        query_lin, key_lin, value_lin, log_decay.T, out_gate, norm_gain.reshape(1, width), state_in,
        query_soft, key_soft, value_soft,
    )
    return pl.pallas_call(
        hand_over,
        out_shape=shapes,
        in_specs=[hbm, hbm, hbm],
        out_specs=(hbm, hbm, hbm),
        scratch_shapes=[
            pltpu.VMEM((rows, width), BF16),
            pltpu.VMEM(state_in.shape, F32),
            pltpu.VMEM((rows, width), BF16),
            dma((2, 9)),
        ],
        compiler_params=pltpu.CompilerParams(vmem_limit_bytes=62 * 2**20),
        name="hand_over",
    )(*results)


def solution(mesh):
    rows = P(("dp", "seq"), None)
    states = P(("dp", "seq"), None, None)
    return jax.shard_map(
        shards,
        mesh=mesh,
        in_specs=(rows, rows, rows, rows, rows, P(), states, rows, rows, rows),
        out_specs=(rows, states, rows),
        check_vma=False,
    )
```

```python
import functools
import math

import jax
import jax.numpy as jnp
from jax import lax
from jax.experimental import pallas as pl
from jax.experimental.pallas import tpu as pltpu
from jax.sharding import PartitionSpec as P

DH = 128
NZ = 8
LHEADS = 32
NORM_EPS = 1e-6
SCALE = DH ** (-0.5)
EXP2_SCALE = SCALE * math.log2(math.e)
MASKED = -1e30
MESH = pl.DeviceIdType.MESH
F32 = jnp.float32
BF16 = jnp.bfloat16
UNROLL = 4
ROWS_BY_ROWS = (((1,), (1,)), ((), ()))
COLS_BY_COLS = (((0,), (0,)), ((), ()))
Z_ORDER = (4, 3, 5, 2, 6, 1, 7)


def place(x, z, c):
    return (x * NZ + z) * 2 + c


def block(index):
    return pl.ds(pl.multiple_of(index * DH, DH), DH)


def wide(index, width):
    return pl.ds(pl.multiple_of(index * width, width), width)


def kernel(
    ql_in, kl_in, vl_in, ld_hbm, gate_in, gain_in, state_in, q_in, k_in, v_in,
    light_out, state_out, attn_out,
    kv, qx, acc, top, low, ob, vsv, vtl,
    qlv, klv, vlv, gtv, lin, ct, cv, s_own, s_oth, s_par, ssend, sgot, eout, egot, ent, esend, gf,
    stin, t0, fin, dt, chd, sq, ld_in,
    lsem, kvs, kvr, qsend, qrecv, st_s, st_r, d_s, d_r, sp_s, sp_r, cd_s, cd_r, sa_s, sa_r,
    eo_s, eo_r, t_s, t_r, so_s, so_r, ep_s, ep_r, ag_s, ag_r, o_s, o_r, out_s,
):
    me = lax.axis_index("seq")
    x = me // (2 * NZ)
    z = (me // 2) % NZ
    c = me % 2
    quad = x * 2 + c
    mates = {1: (x, 1 - c), 2: (1 - x, c), 3: (1 - x, 1 - c)}

    def mate_quad(p):
        mx, mc = mates[p]
        return mx * 2 + mc

    def mate_at(p):
        mx, mc = mates[p]
        return place(mx, z, mc)

    def up(k):
        return (z + k) % NZ

    def remote(src, dst, send, recv, to):
        return pltpu.make_async_remote_copy(
            src_ref=src, dst_ref=dst, send_sem=send, recv_sem=recv,
            device_id={"seq": to}, device_id_type=MESH,
        )

    sends = []

    def go(copy):
        copy.start()
        sends.append(copy)

    barrier = pltpu.get_barrier_semaphore()
    peers = [mate_at(p) for p in (1, 2, 3)] + [place(x, up(k), c) for k in range(1, NZ)]
    for peer in peers:
        pl.semaphore_signal(barrier, inc=1, device_id={"seq": peer}, device_id_type=MESH)

    loads = [
        pltpu.make_async_copy(v_in, vsv, lsem.at[0]),
        pltpu.make_async_copy(kl_in, klv, lsem.at[1]),
        pltpu.make_async_copy(vl_in, vlv, lsem.at[2]),
        pltpu.make_async_copy(ql_in, qlv, lsem.at[3]),
        pltpu.make_async_copy(gate_in, gtv, lsem.at[4]),
        pltpu.make_async_copy(ld_hbm, ld_in, lsem.at[5]),
    ]
    for i in (5, 0, 1, 2, 3, 4):
        loads[i].start()
    loads[5].wait()

    def head_of(n, parity):
        return 16 * (n % 2) + 2 * (n // 2) + parity

    t_row = lax.broadcasted_iota(jnp.int32, (DH, DH), 0)
    t_col = lax.broadcasted_iota(jnp.int32, (DH, DH), 1)
    triu = jnp.where(t_row <= t_col, 1.0, 0.0).astype(BF16)
    cum_t = jnp.dot(ld_in[...], triu, preferred_element_type=F32)
    ct[...] = cum_t
    cv[...] = jnp.transpose(cum_t)
    dt[c] = jnp.broadcast_to(cum_t[:, DH - 1 :], (LHEADS, DH))

    loads[0].wait()
    for g in range(8):
        vtl[g] = jnp.transpose(vsv[:, g * DH : (g + 1) * DH])

    pl.semaphore_wait(barrier, len(peers))

    def kv_quad(hh, sel, p):
        head = mate_quad(p) * 2 + hh
        src = vtl.at[head] if sel else k_in.at[:, block(head)]
        return remote(
            src, kv.at[z, hh, x, sel, block(c), :], kvs.at[hh, sel, p], kvr.at[hh, sel, p], mate_at(p)
        )

    def kv_quad_got(hh, sel, p):
        head = mate_quad(p) * 2 + hh
        src = vtl.at[head] if sel else k_in.at[:, block(head)]
        mx, mc = mates[p]
        return remote(
            src, kv.at[z, hh, mx, sel, block(mc), :], kvs.at[hh, sel, p], kvr.at[hh, sel, p], mate_at(p)
        )

    def kv_own(hh, sel):
        head = quad * 2 + hh
        src = vtl.at[head] if sel else k_in.at[:, block(head)]
        return pltpu.make_async_copy(src, kv.at[z, hh, x, sel, block(c), :], kvr.at[hh, sel, 0])

    for hh in range(2):
        for sel in range(2):
            go(kv_quad(hh, sel, 1))
            kv_own(hh, sel).start()
    for hh in range(2):
        for p in (2, 3):
            for sel in range(2):
                go(kv_quad(hh, sel, p))
    go(remote(dt.at[c], dt.at[c], d_s, d_r, mate_at(1)))

    def ring(hh, way, step, half):
        slot = (z + (NZ - step if way == 0 else step)) % NZ
        to = place(x, up(1 if way == 0 else NZ - 1), c)
        piece = kv.at[slot, hh, x if half == 0 else 1 - x]
        return remote(piece, piece, ag_s.at[hh, way, step, half], ag_r.at[hh, way, step, half], to)

    def ring_got(hh, way, distance, half):
        slot = (z + (NZ - distance if way == 0 else distance)) % NZ
        to = place(x, up(1 if way == 0 else NZ - 1), c)
        piece = kv.at[slot, hh, x if half == 0 else 1 - x]
        step = distance - 1
        return remote(piece, piece, ag_s.at[hh, way, step, half], ag_r.at[hh, way, step, half], to)

    def reach(way, half):
        return 4 if way == half else 3

    def later(half):
        return (x == 1) if half == 0 else (x == 0)

    def goes(way, step, half):
        if way == 0:
            needed = jnp.logical_and(z >= step, z < NZ - 1)
        else:
            needed = (z + step) % NZ < reach(way, half)
        return jnp.logical_or(jnp.logical_not(later(half)), needed)

    def comes(way, distance, half):
        if way == 0:
            needed = z >= distance
        else:
            needed = (z + distance) % NZ < reach(way, half)
        return jnp.logical_or(jnp.logical_not(later(half)), needed)

    ring_sends = []

    def go_ring(hh, way, step, half):
        @pl.when(goes(way, step, half))
        def _():
            ring(hh, way, step, half).start()

        ring_sends.append((hh, way, step, half))

    def start_ring(hh, half):
        for sel in range(2):
            if half == 0:
                kv_own(hh, sel).wait()
                kv_quad_got(hh, sel, 1).wait_recv()
            else:
                kv_quad_got(hh, sel, 2).wait_recv()
                kv_quad_got(hh, sel, 3).wait_recv()
        for way in range(2):
            go_ring(hh, way, 0, half)

    def pump(hh, distance):
        for half in range(2):
            for way in range(2):
                if distance <= reach(way, half):
                    @pl.when(comes(way, distance, half))
                    def _():
                        ring_got(hh, way, distance, half).wait_recv()

                    if distance < reach(way, half):
                        go_ring(hh, way, distance, half)

    def column(h):
        lanes = lax.broadcasted_iota(jnp.int32, (DH, LHEADS), 1)
        return jnp.sum(jnp.where(lanes == h, cv[...], 0.0), axis=1, keepdims=True)

    def silu(u):
        return u / (1.0 + jnp.exp(-u))

    def block_states(parity, target):
        def step(n, carry):
            h = head_of(n, parity)
            keys = (silu(klv[:, block(h)].astype(F32)) * SCALE).astype(BF16)
            klv[:, block(h)] = keys
            col = column(h)
            decayed = (keys.astype(F32) * jnp.exp(col[DH - 1 :, :] - col)).astype(BF16)
            state = lax.dot_general(
                decayed, vlv[:, block(h)], COLS_BY_COLS, preferred_element_type=F32
            )
            target[n] = state.astype(target.dtype)
            return carry

        lax.fori_loop(0, 16, step, 0, unroll=8)

    start_ring(0, 0)
    start_ring(1, 0)
    loads[1].wait()
    loads[2].wait()
    block_states(1 - c, s_oth)
    go(remote(s_oth, s_par, sp_s, sp_r, mate_at(1)))
    start_ring(0, 1)
    block_states(c, s_own)
    start_ring(1, 1)

    def q_quad(hh, p):
        return remote(
            q_in.at[:, wide(mate_quad(p) * 2 + hh, 512)], qx.at[hh, quad],
            qsend.at[hh, p], qrecv.at[hh, p], mate_at(p),
        )

    def q_quad_got(hh, p):
        return remote(
            q_in.at[:, wide(mate_quad(p) * 2 + hh, 512)], qx.at[hh, mate_quad(p)],
            qsend.at[hh, p], qrecv.at[hh, p], mate_at(p),
        )

    def q_own(hh):
        return pltpu.make_async_copy(
            q_in.at[:, wide(quad * 2 + hh, 512)], qx.at[hh, quad], qrecv.at[hh, 0]
        )

    for hh in range(2):
        for p in (2, 3, 1):
            go(q_quad(hh, p))
        q_own(hh).start()

    st_own = pltpu.make_async_copy(state_in.at[0], stin.at[0], st_r.at[0])
    st_move = remote(state_in.at[0], stin.at[1], st_s, st_r.at[1], mate_at(2))

    @pl.when(x == 0)
    def _():
        st_own.start()

    @pl.when(x == 1)
    def _():
        st_move.start()

    remote(dt.at[c], dt.at[1 - c], d_s, d_r, mate_at(1)).wait_recv()
    remote(s_oth, s_par, sp_s, sp_r, mate_at(1)).wait_recv()
    first = c == 0
    chd[z] = jnp.transpose(dt[0] + dt[1])[0:8, :]

    def chip_state(n, carry):
        h = head_of(n, c)
        later = jnp.exp(dt[1, pl.ds(h, 1), :])
        own, par = s_own[n], s_par[n].astype(F32)
        earlier_state = jnp.where(first, own, par)
        later_state = jnp.where(first, par, own)
        ssend[n // 2, n % 2] = (later * earlier_state + later_state).astype(BF16)
        s_own[n] = earlier_state
        return carry

    lax.fori_loop(0, 16, chip_state, 0, unroll=2)
    sgot[z] = ssend[z]

    def chip_decay(k):
        return remote(chd.at[z], chd.at[z], cd_s.at[k - 1], cd_r.at[k - 1], place(x, up(k), c))

    def chip_decay_got(k):
        slot = up(NZ - k)
        return remote(chd.at[slot], chd.at[slot], cd_s.at[k - 1], cd_r.at[k - 1], place(x, up(k), c))

    def state_move(k):
        return remote(
            ssend.at[up(k)], sgot.at[z], sa_s.at[k - 1], sa_r.at[k - 1], place(x, up(k), c)
        )

    def state_got(k):
        return remote(
            ssend.at[up(k)], sgot.at[up(NZ - k)], sa_s.at[k - 1], sa_r.at[k - 1], place(x, up(k), c)
        )

    for k in Z_ORDER:
        go(chip_decay(k))
        go(state_move(k))

    def attend(hh, half, j, slot, both, own):
        heads = pl.ds(pl.multiple_of(j * DH, DH), DH)
        queries = jnp.concatenate([qx[hh, 2 * half, :, heads], qx[hh, 2 * half + 1, :, heads]], axis=0)
        parts = (0, 1) if both else (0,)
        row = pl.ds(half * 4 + j, 1)
        scores = [
            lax.dot_general(kv[slot, hh, i, 0], queries, ROWS_BY_ROWS, preferred_element_type=F32)
            for i in parts
        ]
        if own:
            key = lax.broadcasted_iota(jnp.int32, (2 * DH, 2 * DH), 0)
            query = lax.broadcasted_iota(jnp.int32, (2 * DH, 2 * DH), 1)
            scores[-1] = jnp.where(key <= query, scores[-1], MASKED)
        new = functools.reduce(jnp.maximum, [jnp.max(s, axis=0, keepdims=True) for s in scores])
        if not own:
            old = top[hh, row, :]
            new = jnp.maximum(old, new)
        part, summed = None, None
        for i, s in zip(parts, scores):
            raised = jnp.exp2((s - new) * EXP2_SCALE)
            values = jnp.concatenate([kv[slot, hh, i, 1, :DH, :], kv[slot, hh, i, 1, DH:, :]], axis=1)
            more = jnp.sum(raised, axis=0, keepdims=True)
            product = jnp.dot(values, raised.astype(BF16), preferred_element_type=F32)
            part = more if part is None else part + more
            summed = product if summed is None else summed + product
        if own:
            low[hh, row, :] = part
            acc[hh, half, j] = summed
        else:
            fade = jnp.exp2((old - new) * EXP2_SCALE)
            low[hh, row, :] = low[hh, row, :] * fade + part
            acc[hh, half, j] = acc[hh, half, j] * fade + summed
        top[hh, row, :] = new

    def over_heads(body):
        def step(j, carry):
            body(j)
            return carry

        lax.fori_loop(0, 4, step, 0, unroll=UNROLL)

    def own_slot(hh):
        def body(j):
            attend(hh, 0, j, z, False, True)
            attend(hh, 1, j, z, True, True)

        over_heads(body)

    def other_slot(hh, slot):
        @pl.when(slot < z)
        def _():
            def body(j):
                attend(hh, 0, j, slot, False, False)
                attend(hh, 1, j, slot, True, False)

            over_heads(body)

        @pl.when(slot > z)
        def _():
            over_heads(lambda j: attend(hh, 1, j, slot, False, False))

    def process(hh, distance):
        if distance < 4:
            def step(way, carry):
                other_slot(hh, (z + NZ - distance + 2 * distance * way) % NZ)
                return carry

            lax.fori_loop(0, 2, step, 0)
        else:
            other_slot(hh, (z + distance) % NZ)

    def finish_heads(hh):
        for half, mates_now in ((1 - x, (2, 3)), (x, (1,))):
            def step(j, carry):
                scale = 1.0 / low[hh, pl.ds(half * 4 + j, 1), :]
                result = jnp.transpose(acc[hh, half, j] * scale).astype(BF16)
                ob[hh, 2 * half, :, block(j)] = result[0:DH]
                ob[hh, 2 * half + 1, :, block(j)] = result[DH:]
                return carry

            lax.fori_loop(0, 4, step, 0, unroll=2)
            for p in mates_now:
                go(out_quad(hh, p))
        out_own(hh).start()

    def out_quad(hh, p):
        return remote(
            ob.at[hh, mate_quad(p)], attn_out.at[:, wide(quad * 2 + hh, 512)],
            o_s.at[hh, p], o_r.at[hh, p], mate_at(p),
        )

    def out_got(hh, p):
        return remote(
            ob.at[hh, mate_quad(p)], attn_out.at[:, wide(mate_quad(p) * 2 + hh, 512)],
            o_s.at[hh, p], o_r.at[hh, p], mate_at(p),
        )

    def out_own(hh):
        return pltpu.make_async_copy(
            ob.at[hh, quad], attn_out.at[:, wide(quad * 2 + hh, 512)], o_r.at[hh, 0]
        )

    def queries_here(hh):
        q_own(hh).wait()
        for p in (1, 2, 3):
            q_quad_got(hh, p).wait_recv()

    def inner_heads(begin, end):
        def step(h, carry):
            queries = silu(qlv[:, block(h)].astype(F32)).astype(BF16)
            qlv[:, block(h)] = queries
            scores = lax.dot_general(
                queries, klv[:, block(h)], ROWS_BY_ROWS, preferred_element_type=F32
            )
            spread = column(h) - ct[pl.ds(h, 1), :]
            damping = jnp.exp(jnp.where(t_row >= t_col, spread, MASKED))
            damped = (scores * damping).astype(BF16)
            lin[:, block(h)] = jnp.dot(damped, vlv[:, block(h)], preferred_element_type=F32)
            return carry

        lax.fori_loop(begin, end, step, 0, unroll=8)

    t_move = remote(fin, t0, t_s, t_r, mate_at(2))
    so_move = remote(fin.at[0], state_out.at[0], so_s, so_r.at[0], mate_at(2))
    so_own = pltpu.make_async_copy(fin.at[1], state_out.at[0], so_r.at[1])

    def enter_move(k, part):
        return remote(
            eout.at[up(k), part], egot.at[z, part],
            eo_s.at[part, k - 1], eo_r.at[part, k - 1], place(x, up(k), c),
        )

    def enter_got(k, part):
        return remote(
            eout.at[up(k), part], egot.at[up(NZ - k), part],
            eo_s.at[part, k - 1], eo_r.at[part, k - 1], place(x, up(k), c),
        )

    def prefix():
        lanes = lax.broadcasted_iota(jnp.int32, (8, LHEADS), 1)
        for k in range(2):
            state = fin[k]
            for zi in range(NZ):
                eout[zi, k] = state.astype(BF16)
                total = jnp.where(lanes == 16 * k + 2 * z + c, chd[zi], 0.0)
                decay = jnp.exp(jnp.sum(total, axis=1, keepdims=True))[0:1, :]
                state = decay * state + sgot[zi, k].astype(F32)
            fin[k] = state

    def states_here():
        for k in Z_ORDER:
            chip_decay_got(k).wait_recv()
            state_got(k).wait_recv()

    def owner_0():
        @pl.when(x == 0)
        def _():
            st_own.wait()
            st_move.wait_recv()
            fin[...] = stin[...]
            prefix()
            t_move.start()

    def owner_1():
        @pl.when(x == 1)
        def _():
            t_move.wait_recv()
            fin[...] = t0[...]
            prefix()
            so_move.start()
            so_own.start()

    def enter_send(part):
        for k in Z_ORDER:
            go(enter_move(k, part))
        egot[z, part] = eout[z, part]

    def pair_enter(part):
        for k in Z_ORDER:
            enter_got(k, part).wait_recv()

        def step(zi, carry):
            h = 16 * part + 2 * zi + c
            entering = egot[zi, part]
            after = jnp.exp(dt[0, pl.ds(h, 1), :]) * entering.astype(F32) + s_own[2 * zi + part]
            after = after.astype(BF16)
            ent[c, part, zi] = jnp.where(first, entering, after)
            esend[part, zi] = jnp.where(first, after, entering)
            return carry

        lax.fori_loop(0, NZ, step, 0, unroll=2)
        go(enter_pair(part))

    def enter_pair(part):
        return remote(esend.at[part], ent.at[c, part], ep_s.at[part], ep_r.at[part], mate_at(1))

    def enter_pair_got(part):
        return remote(esend.at[part], ent.at[1 - c, part], ep_s.at[part], ep_r.at[part], mate_at(1))

    def carried(parity, part):
        def step(zi, carry):
            h = 16 * part + 2 * zi + parity
            reached = jnp.dot(qlv[:, block(h)], ent[parity, part, zi], preferred_element_type=F32)
            mixed = lin[:, block(h)] + jnp.exp(column(h)) * reached
            lin[:, block(h)] = mixed
            sq[...] += mixed * mixed
            return carry

        lax.fori_loop(0, NZ, step, 0, unroll=4)

    def gates():
        def step(h, carry):
            gate = 1.0 / (1.0 + jnp.exp(-gtv[:, block(h)].astype(F32)))
            gf[:, block(h)] = gain_in[:, block(h)] * gate
            return carry

        lax.fori_loop(0, LHEADS, step, 0, unroll=4)

    def gated_heads():
        mean = jnp.sum(sq[...], axis=1, keepdims=True) / (LHEADS * DH)
        factor = jnp.broadcast_to(lax.rsqrt(mean + NORM_EPS), (DH, DH))

        def gated(h, carry):
            qlv[:, block(h)] = (lin[:, block(h)] * factor * gf[:, block(h)]).astype(BF16)
            return carry

        lax.fori_loop(0, LHEADS, gated, 0, unroll=4)
        light_copy.start()

    light_copy = pltpu.make_async_copy(qlv, light_out, out_s)

    loads[3].wait()
    inner_heads(0, 16)
    pump(0, 1)
    inner_heads(16, 32)
    pump(1, 1)
    loads[4].wait()
    gates()
    queries_here(0)
    own_slot(0)
    process(0, 1)
    queries_here(1)
    pump(0, 2)
    own_slot(1)
    states_here()
    owner_0()
    pump(1, 2)
    process(1, 1)
    owner_1()
    pump(0, 3)
    enter_send(0)
    process(0, 2)
    process(1, 2)
    pump(1, 3)
    enter_send(1)
    process(0, 3)
    pump(0, 4)
    process(0, 4)
    finish_heads(0)
    process(1, 3)
    pump(1, 4)
    process(1, 4)
    finish_heads(1)
    pair_enter(0)
    sq[...] = jnp.zeros_like(sq)
    carried(c, 0)
    enter_pair_got(0).wait_recv()
    carried(1 - c, 0)
    pair_enter(1)
    carried(c, 1)
    enter_pair_got(1).wait_recv()
    carried(1 - c, 1)
    gated_heads()

    for hh in range(2):
        out_own(hh).wait()
        for p in (1, 2, 3):
            out_got(hh, p).wait_recv()
    light_copy.wait()

    @pl.when(x == 0)
    def _():
        so_move.wait_recv()
        t_move.wait_send()

    @pl.when(x == 1)
    def _():
        st_move.wait_send()
        so_own.wait()
        so_move.wait_send()

    for copy in sends:
        copy.wait_send()
    for hh, way, step, half in ring_sends:
        @pl.when(goes(way, step, half))
        def _():
            ring(hh, way, step, half).wait_send()


def hand_over(light_in, state_in, attn_in, light_out, state_out, attn_out, light, state, attn, sem):
    rows = light.shape[0] // 4
    moves = [(state_in, state, state_out)]
    for i in range(4):
        part = pl.ds(i * rows, rows)
        moves.append((light_in.at[part, :], light.at[part, :], light_out.at[part, :]))
        moves.append((attn_in.at[part, :], attn.at[part, :], attn_out.at[part, :]))
    into = [pltpu.make_async_copy(a, b, sem.at[0, i]) for i, (a, b, _) in enumerate(moves)]
    out = [pltpu.make_async_copy(b, a, sem.at[1, i]) for i, (_, b, a) in enumerate(moves)]
    for copy in into:
        copy.start()
    for i in range(len(moves)):
        into[i].wait()
        out[i].start()
    for copy in out:
        copy.wait()


def shards(*arrays):
    (query_lin, key_lin, value_lin, log_decay, out_gate, norm_gain, state_in, query_soft, key_soft,
     value_soft) = arrays
    rows, width = query_lin.shape
    hbm = pl.BlockSpec(memory_space=pl.ANY)
    vmem = pl.BlockSpec(memory_space=pltpu.VMEM)
    dma = pltpu.SemaphoreType.DMA
    state = (DH, DH)
    shapes = (
        jax.ShapeDtypeStruct((rows, width), BF16),
        jax.ShapeDtypeStruct(state_in.shape, F32),
        jax.ShapeDtypeStruct((rows, width), BF16),
    )
    results = pl.pallas_call(
        kernel,
        out_shape=shapes,
        in_specs=[hbm, hbm, hbm, hbm, hbm, vmem, hbm, hbm, hbm, hbm],
        out_specs=(hbm, hbm, hbm),
        scratch_shapes=[
            pltpu.VMEM((NZ, 2, 2, 2, 2 * DH, DH), BF16),
            pltpu.VMEM((2, 4, rows, 512), BF16),
            pltpu.VMEM((2, 2, 4, DH, 2 * DH), F32),
            pltpu.VMEM((2, 8, 2 * DH), F32),
            pltpu.VMEM((2, 8, 2 * DH), F32),
            pltpu.VMEM((2, 4, rows, 512), BF16),
            pltpu.VMEM((rows, 1024), BF16),
            pltpu.VMEM((8, DH, rows), BF16),
            pltpu.VMEM((rows, width), BF16),
            pltpu.VMEM((rows, width), BF16),
            pltpu.VMEM((rows, width), BF16),
            pltpu.VMEM((rows, width), BF16),
            pltpu.VMEM((rows, width), F32),
            pltpu.VMEM((LHEADS, DH), F32),
            pltpu.VMEM((DH, LHEADS), F32),
            pltpu.VMEM((16,) + state, F32),
            pltpu.VMEM((16,) + state, BF16),
            pltpu.VMEM((16,) + state, BF16),
            pltpu.VMEM((NZ, 2) + state, BF16),
            pltpu.VMEM((NZ, 2) + state, BF16),
            pltpu.VMEM((NZ, 2) + state, BF16),
            pltpu.VMEM((NZ, 2) + state, BF16),
            pltpu.VMEM((2, 2, NZ) + state, BF16),
            pltpu.VMEM((2, NZ) + state, BF16),
            pltpu.VMEM((rows, width), F32),
            pltpu.VMEM((2,) + state, F32),
            pltpu.VMEM((2,) + state, F32),
            pltpu.VMEM((2,) + state, F32),
            pltpu.VMEM((2, LHEADS, DH), F32),
            pltpu.VMEM((NZ, 8, LHEADS), F32),
            pltpu.VMEM(state, F32),
            pltpu.VMEM((LHEADS, rows), BF16),
            dma((6,)),
            dma((2, 2, 4)), dma((2, 2, 4)),
            dma((2, 4)), dma((2, 4)),
            dma, dma((2,)),
            dma, dma,
            dma, dma,
            dma((7,)), dma((7,)),
            dma((7,)), dma((7,)),
            dma((2, 7)), dma((2, 7)),
            dma, dma,
            dma, dma((2,)),
            dma((2,)), dma((2,)),
            dma((2, 2, 4, 2)), dma((2, 2, 4, 2)),
            dma((2, 4)), dma((2, 4)),
            dma,
        ],
        compiler_params=pltpu.CompilerParams(
            collective_id=0, has_side_effects=True, vmem_limit_bytes=62 * 2**20
        ),
        name="window",
    )(
        query_lin, key_lin, value_lin, log_decay.T, out_gate, norm_gain.reshape(1, width), state_in,
        query_soft, key_soft, value_soft,
    )
    return pl.pallas_call(
        hand_over,
        out_shape=shapes,
        in_specs=[hbm, hbm, hbm],
        out_specs=(hbm, hbm, hbm),
        scratch_shapes=[
            pltpu.VMEM((rows, width), BF16),
            pltpu.VMEM(state_in.shape, F32),
            pltpu.VMEM((rows, width), BF16),
            dma((2, 9)),
        ],
        compiler_params=pltpu.CompilerParams(vmem_limit_bytes=62 * 2**20),
        name="hand_over",
    )(*results)


def solution(mesh):
    rows = P(("dp", "seq"), None)
    states = P(("dp", "seq"), None, None)
    return jax.shard_map(
        shards,
        mesh=mesh,
        in_specs=(rows, rows, rows, rows, rows, P(), states, rows, rows, rows),
        out_specs=(rows, states, rows),
        check_vma=False,
    )
```

```python
import functools
import math

import jax
import jax.numpy as jnp
from jax import lax
from jax.experimental import pallas as pl
from jax.experimental.pallas import tpu as pltpu
from jax.sharding import PartitionSpec as P

DH = 128
NZ = 8
LHEADS = 32
NORM_EPS = 1e-6
SCALE = DH ** (-0.5)
EXP2_SCALE = SCALE * math.log2(math.e)
MASKED = -1e30
MESH = pl.DeviceIdType.MESH
F32 = jnp.float32
BF16 = jnp.bfloat16
UNROLL = 4
ROWS_BY_ROWS = (((1,), (1,)), ((), ()))
COLS_BY_COLS = (((0,), (0,)), ((), ()))
Z_ORDER = (4, 3, 5, 2, 6, 1, 7)


def place(x, z, c):
    return (x * NZ + z) * 2 + c


def block(index):
    return pl.ds(pl.multiple_of(index * DH, DH), DH)


def wide(index, width):
    return pl.ds(pl.multiple_of(index * width, width), width)


def kernel(
    ql_in, kl_in, vl_in, ld_hbm, gate_in, gain_in, state_in, q_in, k_in, v_in,
    light_out, state_out, attn_out,
    kv, qx, acc, top, low, ob, vsv, vtl,
    qlv, klv, vlv, gtv, lin, ct, cv, s_own, s_oth, s_par, ssend, sgot, eout, egot, ent, esend, gf,
    stin, t0, fin, dt, chd, sq, ld_in,
    lsem, kvs, kvr, qsend, qrecv, st_s, st_r, d_s, d_r, sp_s, sp_r, cd_s, cd_r, sa_s, sa_r,
    eo_s, eo_r, t_s, t_r, so_s, so_r, ep_s, ep_r, ag_s, ag_r, o_s, o_r, out_s,
):
    me = lax.axis_index("seq")
    x = me // (2 * NZ)
    z = (me // 2) % NZ
    c = me % 2
    quad = x * 2 + c
    mates = {1: (x, 1 - c), 2: (1 - x, c), 3: (1 - x, 1 - c)}

    def mate_quad(p):
        mx, mc = mates[p]
        return mx * 2 + mc

    def mate_at(p):
        mx, mc = mates[p]
        return place(mx, z, mc)

    def up(k):
        return (z + k) % NZ

    def remote(src, dst, send, recv, to):
        return pltpu.make_async_remote_copy(
            src_ref=src, dst_ref=dst, send_sem=send, recv_sem=recv,
            device_id={"seq": to}, device_id_type=MESH,
        )

    sends = []

    def go(copy):
        copy.start()
        sends.append(copy)

    barrier = pltpu.get_barrier_semaphore()
    peers = [mate_at(p) for p in (1, 2, 3)] + [place(x, up(k), c) for k in range(1, NZ)]
    for peer in peers:
        pl.semaphore_signal(barrier, inc=1, device_id={"seq": peer}, device_id_type=MESH)

    loads = [
        pltpu.make_async_copy(v_in, vsv, lsem.at[0]),
        pltpu.make_async_copy(kl_in, klv, lsem.at[1]),
        pltpu.make_async_copy(vl_in, vlv, lsem.at[2]),
        pltpu.make_async_copy(ql_in, qlv, lsem.at[3]),
        pltpu.make_async_copy(gate_in, gtv, lsem.at[4]),
        pltpu.make_async_copy(ld_hbm, ld_in, lsem.at[5]),
    ]
    for i in (5, 0, 1, 2, 3, 4):
        loads[i].start()
    loads[5].wait()

    def head_of(n, parity):
        return 16 * (n % 2) + 2 * (n // 2) + parity

    t_row = lax.broadcasted_iota(jnp.int32, (DH, DH), 0)
    t_col = lax.broadcasted_iota(jnp.int32, (DH, DH), 1)
    triu = jnp.where(t_row <= t_col, 1.0, 0.0).astype(BF16)
    cum_t = jnp.dot(ld_in[...], triu, preferred_element_type=F32)
    ct[...] = cum_t
    cv[...] = jnp.transpose(cum_t)
    dt[c] = jnp.broadcast_to(cum_t[:, DH - 1 :], (LHEADS, DH))

    loads[0].wait()
    for g in range(8):
        vtl[g] = jnp.transpose(vsv[:, g * DH : (g + 1) * DH])

    pl.semaphore_wait(barrier, len(peers))

    def kv_quad(hh, sel, p):
        head = mate_quad(p) * 2 + hh
        src = vtl.at[head] if sel else k_in.at[:, block(head)]
        return remote(
            src, kv.at[z, hh, x, sel, block(c), :], kvs.at[hh, sel, p], kvr.at[hh, sel, p], mate_at(p)
        )

    def kv_quad_got(hh, sel, p):
        head = mate_quad(p) * 2 + hh
        src = vtl.at[head] if sel else k_in.at[:, block(head)]
        mx, mc = mates[p]
        return remote(
            src, kv.at[z, hh, mx, sel, block(mc), :], kvs.at[hh, sel, p], kvr.at[hh, sel, p], mate_at(p)
        )

    def kv_own(hh, sel):
        head = quad * 2 + hh
        src = vtl.at[head] if sel else k_in.at[:, block(head)]
        return pltpu.make_async_copy(src, kv.at[z, hh, x, sel, block(c), :], kvr.at[hh, sel, 0])

    for hh in range(2):
        for sel in range(2):
            go(kv_quad(hh, sel, 1))
            kv_own(hh, sel).start()
    for hh in range(2):
        for p in (2, 3):
            for sel in range(2):
                go(kv_quad(hh, sel, p))
    go(remote(dt.at[c], dt.at[c], d_s, d_r, mate_at(1)))

    def ring(hh, way, step, half):
        slot = (z + (NZ - step if way == 0 else step)) % NZ
        to = place(x, up(1 if way == 0 else NZ - 1), c)
        piece = kv.at[slot, hh, x if half == 0 else 1 - x]
        return remote(piece, piece, ag_s.at[hh, way, step, half], ag_r.at[hh, way, step, half], to)

    def ring_got(hh, way, distance, half):
        slot = (z + (NZ - distance if way == 0 else distance)) % NZ
        to = place(x, up(1 if way == 0 else NZ - 1), c)
        piece = kv.at[slot, hh, x if half == 0 else 1 - x]
        step = distance - 1
        return remote(piece, piece, ag_s.at[hh, way, step, half], ag_r.at[hh, way, step, half], to)

    def reach(way, half):
        return 4 if way == half else 3

    def later(half):
        return (x == 1) if half == 0 else (x == 0)

    def goes(way, step, half):
        if way == 0:
            needed = jnp.logical_and(z >= step, z < NZ - 1)
        else:
            needed = (z + step) % NZ < reach(way, half)
        return jnp.logical_or(jnp.logical_not(later(half)), needed)

    def comes(way, distance, half):
        if way == 0:
            needed = z >= distance
        else:
            needed = (z + distance) % NZ < reach(way, half)
        return jnp.logical_or(jnp.logical_not(later(half)), needed)

    ring_sends = []

    def go_ring(hh, way, step, half):
        @pl.when(goes(way, step, half))
        def _():
            ring(hh, way, step, half).start()

        ring_sends.append((hh, way, step, half))

    def start_ring(hh, half):
        for sel in range(2):
            if half == 0:
                kv_own(hh, sel).wait()
                kv_quad_got(hh, sel, 1).wait_recv()
            else:
                kv_quad_got(hh, sel, 2).wait_recv()
                kv_quad_got(hh, sel, 3).wait_recv()
        for way in range(2):
            go_ring(hh, way, 0, half)

    def pump(hh, distance):
        for half in range(2):
            for way in range(2):
                if distance <= reach(way, half):
                    @pl.when(comes(way, distance, half))
                    def _():
                        ring_got(hh, way, distance, half).wait_recv()

                    if distance < reach(way, half):
                        go_ring(hh, way, distance, half)

    def column(h):
        lanes = lax.broadcasted_iota(jnp.int32, (DH, LHEADS), 1)
        return jnp.sum(jnp.where(lanes == h, cv[...], 0.0), axis=1, keepdims=True)

    def silu(u):
        return u / (1.0 + jnp.exp(-u))

    def block_states(parity, target):
        def step(n, carry):
            h = head_of(n, parity)
            keys = (silu(klv[:, block(h)].astype(F32)) * SCALE).astype(BF16)
            klv[:, block(h)] = keys
            col = column(h)
            decayed = (keys.astype(F32) * jnp.exp(col[DH - 1 :, :] - col)).astype(BF16)
            state = lax.dot_general(
                decayed, vlv[:, block(h)], COLS_BY_COLS, preferred_element_type=F32
            )
            target[n] = state.astype(target.dtype)
            return carry

        lax.fori_loop(0, 16, step, 0, unroll=8)

    start_ring(0, 0)
    start_ring(1, 0)
    loads[1].wait()
    loads[2].wait()
    block_states(1 - c, s_oth)
    go(remote(s_oth, s_par, sp_s, sp_r, mate_at(1)))
    start_ring(0, 1)
    block_states(c, s_own)
    start_ring(1, 1)

    def q_quad(hh, p):
        return remote(
            q_in.at[:, wide(mate_quad(p) * 2 + hh, 512)], qx.at[hh, quad],
            qsend.at[hh, p], qrecv.at[hh, p], mate_at(p),
        )

    def q_quad_got(hh, p):
        return remote(
            q_in.at[:, wide(mate_quad(p) * 2 + hh, 512)], qx.at[hh, mate_quad(p)],
            qsend.at[hh, p], qrecv.at[hh, p], mate_at(p),
        )

    def q_own(hh):
        return pltpu.make_async_copy(
            q_in.at[:, wide(quad * 2 + hh, 512)], qx.at[hh, quad], qrecv.at[hh, 0]
        )

    for hh in range(2):
        for p in (2, 3, 1):
            go(q_quad(hh, p))
        q_own(hh).start()

    st_own = pltpu.make_async_copy(state_in.at[0], stin.at[0], st_r.at[0])
    st_move = remote(state_in.at[0], stin.at[1], st_s, st_r.at[1], mate_at(2))

    @pl.when(x == 0)
    def _():
        st_own.start()

    @pl.when(x == 1)
    def _():
        st_move.start()

    remote(dt.at[c], dt.at[1 - c], d_s, d_r, mate_at(1)).wait_recv()
    remote(s_oth, s_par, sp_s, sp_r, mate_at(1)).wait_recv()
    first = c == 0
    chd[z] = jnp.transpose(dt[0] + dt[1])[0:8, :]

    def chip_state(n, carry):
        h = head_of(n, c)
        later = jnp.exp(dt[1, pl.ds(h, 1), :])
        own, par = s_own[n], s_par[n].astype(F32)
        earlier_state = jnp.where(first, own, par)
        later_state = jnp.where(first, par, own)
        ssend[n // 2, n % 2] = (later * earlier_state + later_state).astype(BF16)
        s_own[n] = earlier_state
        return carry

    lax.fori_loop(0, 16, chip_state, 0, unroll=4)
    sgot[z] = ssend[z]

    def chip_decay(k):
        return remote(chd.at[z], chd.at[z], cd_s.at[k - 1], cd_r.at[k - 1], place(x, up(k), c))

    def chip_decay_got(k):
        slot = up(NZ - k)
        return remote(chd.at[slot], chd.at[slot], cd_s.at[k - 1], cd_r.at[k - 1], place(x, up(k), c))

    def state_move(k):
        return remote(
            ssend.at[up(k)], sgot.at[z], sa_s.at[k - 1], sa_r.at[k - 1], place(x, up(k), c)
        )

    def state_got(k):
        return remote(
            ssend.at[up(k)], sgot.at[up(NZ - k)], sa_s.at[k - 1], sa_r.at[k - 1], place(x, up(k), c)
        )

    for k in Z_ORDER:
        go(chip_decay(k))
        go(state_move(k))

    def attend(hh, half, j, slot, both, own):
        heads = pl.ds(pl.multiple_of(j * DH, DH), DH)
        queries = jnp.concatenate([qx[hh, 2 * half, :, heads], qx[hh, 2 * half + 1, :, heads]], axis=0)
        parts = (0, 1) if both else (0,)
        row = pl.ds(half * 4 + j, 1)
        scores = [
            lax.dot_general(kv[slot, hh, i, 0], queries, ROWS_BY_ROWS, preferred_element_type=F32)
            for i in parts
        ]
        if own:
            key = lax.broadcasted_iota(jnp.int32, (2 * DH, 2 * DH), 0)
            query = lax.broadcasted_iota(jnp.int32, (2 * DH, 2 * DH), 1)
            scores[-1] = jnp.where(key <= query, scores[-1], MASKED)
        new = functools.reduce(jnp.maximum, [jnp.max(s, axis=0, keepdims=True) for s in scores])
        if not own:
            old = top[hh, row, :]
            new = jnp.maximum(old, new)
        part, summed = None, None
        for i, s in zip(parts, scores):
            raised = jnp.exp2((s - new) * EXP2_SCALE)
            values = jnp.concatenate([kv[slot, hh, i, 1, :DH, :], kv[slot, hh, i, 1, DH:, :]], axis=1)
            more = jnp.sum(raised, axis=0, keepdims=True)
            product = jnp.dot(values, raised.astype(BF16), preferred_element_type=F32)
            part = more if part is None else part + more
            summed = product if summed is None else summed + product
        if own:
            low[hh, row, :] = part
            acc[hh, half, j] = summed
        else:
            fade = jnp.exp2((old - new) * EXP2_SCALE)
            low[hh, row, :] = low[hh, row, :] * fade + part
            acc[hh, half, j] = acc[hh, half, j] * fade + summed
        top[hh, row, :] = new

    def over_heads(body):
        def step(j, carry):
            body(j)
            return carry

        lax.fori_loop(0, 4, step, 0, unroll=UNROLL)

    def own_slot(hh):
        def body(j):
            attend(hh, 0, j, z, False, True)
            attend(hh, 1, j, z, True, True)

        over_heads(body)

    def other_slot(hh, slot):
        @pl.when(slot < z)
        def _():
            def body(j):
                attend(hh, 0, j, slot, False, False)
                attend(hh, 1, j, slot, True, False)

            over_heads(body)

        @pl.when(slot > z)
        def _():
            over_heads(lambda j: attend(hh, 1, j, slot, False, False))

    def process(hh, distance):
        if distance < 4:
            def step(way, carry):
                other_slot(hh, (z + NZ - distance + 2 * distance * way) % NZ)
                return carry

            lax.fori_loop(0, 2, step, 0)
        else:
            other_slot(hh, (z + distance) % NZ)

    def finish_heads(hh):
        for half, mates_now in ((1 - x, (2, 3)), (x, (1,))):
            def step(j, carry):
                scale = 1.0 / low[hh, pl.ds(half * 4 + j, 1), :]
                result = jnp.transpose(acc[hh, half, j] * scale).astype(BF16)
                ob[hh, 2 * half, :, block(j)] = result[0:DH]
                ob[hh, 2 * half + 1, :, block(j)] = result[DH:]
                return carry

            lax.fori_loop(0, 4, step, 0, unroll=4)
            for p in mates_now:
                go(out_quad(hh, p))
        out_own(hh).start()

    def out_quad(hh, p):
        return remote(
            ob.at[hh, mate_quad(p)], attn_out.at[:, wide(quad * 2 + hh, 512)],
            o_s.at[hh, p], o_r.at[hh, p], mate_at(p),
        )

    def out_got(hh, p):
        return remote(
            ob.at[hh, mate_quad(p)], attn_out.at[:, wide(mate_quad(p) * 2 + hh, 512)],
            o_s.at[hh, p], o_r.at[hh, p], mate_at(p),
        )

    def out_own(hh):
        return pltpu.make_async_copy(
            ob.at[hh, quad], attn_out.at[:, wide(quad * 2 + hh, 512)], o_r.at[hh, 0]
        )

    def queries_here(hh):
        q_own(hh).wait()
        for p in (1, 2, 3):
            q_quad_got(hh, p).wait_recv()

    def inner_heads(begin, end):
        def step(h, carry):
            queries = silu(qlv[:, block(h)].astype(F32)).astype(BF16)
            qlv[:, block(h)] = queries
            scores = lax.dot_general(
                queries, klv[:, block(h)], ROWS_BY_ROWS, preferred_element_type=F32
            )
            spread = column(h) - ct[pl.ds(h, 1), :]
            damping = jnp.exp(jnp.where(t_row >= t_col, spread, MASKED))
            damped = (scores * damping).astype(BF16)
            lin[:, block(h)] = jnp.dot(damped, vlv[:, block(h)], preferred_element_type=F32)
            return carry

        lax.fori_loop(begin, end, step, 0, unroll=8)

    t_move = remote(fin, t0, t_s, t_r, mate_at(2))
    so_move = remote(fin.at[0], state_out.at[0], so_s, so_r.at[0], mate_at(2))
    so_own = pltpu.make_async_copy(fin.at[1], state_out.at[0], so_r.at[1])

    def enter_move(k, part):
        return remote(
            eout.at[up(k), part], egot.at[z, part],
            eo_s.at[part, k - 1], eo_r.at[part, k - 1], place(x, up(k), c),
        )

    def enter_got(k, part):
        return remote(
            eout.at[up(k), part], egot.at[up(NZ - k), part],
            eo_s.at[part, k - 1], eo_r.at[part, k - 1], place(x, up(k), c),
        )

    def prefix():
        lanes = lax.broadcasted_iota(jnp.int32, (8, LHEADS), 1)
        for k in range(2):
            state = fin[k]
            for zi in range(NZ):
                eout[zi, k] = state.astype(BF16)
                total = jnp.where(lanes == 16 * k + 2 * z + c, chd[zi], 0.0)
                decay = jnp.exp(jnp.sum(total, axis=1, keepdims=True))[0:1, :]
                state = decay * state + sgot[zi, k].astype(F32)
            fin[k] = state

    def states_here():
        for k in Z_ORDER:
            chip_decay_got(k).wait_recv()
            state_got(k).wait_recv()

    def owner_0():
        @pl.when(x == 0)
        def _():
            st_own.wait()
            st_move.wait_recv()
            fin[...] = stin[...]
            prefix()
            t_move.start()

    def owner_1():
        @pl.when(x == 1)
        def _():
            t_move.wait_recv()
            fin[...] = t0[...]
            prefix()
            so_move.start()
            so_own.start()

    def enter_send(part):
        for k in Z_ORDER:
            go(enter_move(k, part))
        egot[z, part] = eout[z, part]

    def pair_enter(part):
        for k in Z_ORDER:
            enter_got(k, part).wait_recv()

        def step(zi, carry):
            h = 16 * part + 2 * zi + c
            entering = egot[zi, part]
            after = jnp.exp(dt[0, pl.ds(h, 1), :]) * entering.astype(F32) + s_own[2 * zi + part]
            after = after.astype(BF16)
            ent[c, part, zi] = jnp.where(first, entering, after)
            esend[part, zi] = jnp.where(first, after, entering)
            return carry

        lax.fori_loop(0, NZ, step, 0, unroll=4)
        go(enter_pair(part))

    def enter_pair(part):
        return remote(esend.at[part], ent.at[c, part], ep_s.at[part], ep_r.at[part], mate_at(1))

    def enter_pair_got(part):
        return remote(esend.at[part], ent.at[1 - c, part], ep_s.at[part], ep_r.at[part], mate_at(1))

    def carried(parity, part):
        def step(zi, carry):
            h = 16 * part + 2 * zi + parity
            reached = jnp.dot(qlv[:, block(h)], ent[parity, part, zi], preferred_element_type=F32)
            mixed = lin[:, block(h)] + jnp.exp(column(h)) * reached
            lin[:, block(h)] = mixed
            sq[...] += mixed * mixed
            return carry

        lax.fori_loop(0, NZ, step, 0, unroll=8)

    def gates():
        def step(h, carry):
            gate = 1.0 / (1.0 + jnp.exp(-gtv[:, block(h)].astype(F32)))
            gf[:, block(h)] = gain_in[:, block(h)] * gate
            return carry

        lax.fori_loop(0, LHEADS, step, 0, unroll=4)

    def gated_heads():
        mean = jnp.sum(sq[...], axis=1, keepdims=True) / (LHEADS * DH)
        factor = jnp.broadcast_to(lax.rsqrt(mean + NORM_EPS), (DH, DH))

        def gated(h, carry):
            qlv[:, block(h)] = (lin[:, block(h)] * factor * gf[:, block(h)]).astype(BF16)
            return carry

        lax.fori_loop(0, LHEADS, gated, 0, unroll=8)
        light_copy.start()

    light_copy = pltpu.make_async_copy(qlv, light_out, out_s)

    loads[3].wait()
    inner_heads(0, 16)
    pump(0, 1)
    inner_heads(16, 32)
    pump(1, 1)
    loads[4].wait()
    gates()
    queries_here(0)
    own_slot(0)
    process(0, 1)
    queries_here(1)
    pump(0, 2)
    own_slot(1)
    states_here()
    owner_0()
    pump(1, 2)
    process(1, 1)
    owner_1()
    pump(0, 3)
    enter_send(0)
    process(0, 2)
    process(1, 2)
    pump(1, 3)
    enter_send(1)
    process(0, 3)
    pump(0, 4)
    process(0, 4)
    finish_heads(0)
    process(1, 3)
    pump(1, 4)
    process(1, 4)
    finish_heads(1)
    pair_enter(0)
    sq[...] = jnp.zeros_like(sq)
    carried(c, 0)
    enter_pair_got(0).wait_recv()
    carried(1 - c, 0)
    pair_enter(1)
    carried(c, 1)
    enter_pair_got(1).wait_recv()
    carried(1 - c, 1)
    gated_heads()

    for hh in range(2):
        out_own(hh).wait()
        for p in (1, 2, 3):
            out_got(hh, p).wait_recv()
    light_copy.wait()

    @pl.when(x == 0)
    def _():
        so_move.wait_recv()
        t_move.wait_send()

    @pl.when(x == 1)
    def _():
        st_move.wait_send()
        so_own.wait()
        so_move.wait_send()

    for copy in sends:
        copy.wait_send()
    for hh, way, step, half in ring_sends:
        @pl.when(goes(way, step, half))
        def _():
            ring(hh, way, step, half).wait_send()


def hand_over(light_in, state_in, attn_in, light_out, state_out, attn_out, light, state, attn, sem):
    rows = light.shape[0] // 4
    moves = [(state_in, state, state_out)]
    for i in range(4):
        part = pl.ds(i * rows, rows)
        moves.append((light_in.at[part, :], light.at[part, :], light_out.at[part, :]))
        moves.append((attn_in.at[part, :], attn.at[part, :], attn_out.at[part, :]))
    into = [pltpu.make_async_copy(a, b, sem.at[0, i]) for i, (a, b, _) in enumerate(moves)]
    out = [pltpu.make_async_copy(b, a, sem.at[1, i]) for i, (_, b, a) in enumerate(moves)]
    for copy in into:
        copy.start()
    for i in range(len(moves)):
        into[i].wait()
        out[i].start()
    for copy in out:
        copy.wait()


def shards(*arrays):
    (query_lin, key_lin, value_lin, log_decay, out_gate, norm_gain, state_in, query_soft, key_soft,
     value_soft) = arrays
    rows, width = query_lin.shape
    hbm = pl.BlockSpec(memory_space=pl.ANY)
    vmem = pl.BlockSpec(memory_space=pltpu.VMEM)
    dma = pltpu.SemaphoreType.DMA
    state = (DH, DH)
    shapes = (
        jax.ShapeDtypeStruct((rows, width), BF16),
        jax.ShapeDtypeStruct(state_in.shape, F32),
        jax.ShapeDtypeStruct((rows, width), BF16),
    )
    results = pl.pallas_call(
        kernel,
        out_shape=shapes,
        in_specs=[hbm, hbm, hbm, hbm, hbm, vmem, hbm, hbm, hbm, hbm],
        out_specs=(hbm, hbm, hbm),
        scratch_shapes=[
            pltpu.VMEM((NZ, 2, 2, 2, 2 * DH, DH), BF16),
            pltpu.VMEM((2, 4, rows, 512), BF16),
            pltpu.VMEM((2, 2, 4, DH, 2 * DH), F32),
            pltpu.VMEM((2, 8, 2 * DH), F32),
            pltpu.VMEM((2, 8, 2 * DH), F32),
            pltpu.VMEM((2, 4, rows, 512), BF16),
            pltpu.VMEM((rows, 1024), BF16),
            pltpu.VMEM((8, DH, rows), BF16),
            pltpu.VMEM((rows, width), BF16),
            pltpu.VMEM((rows, width), BF16),
            pltpu.VMEM((rows, width), BF16),
            pltpu.VMEM((rows, width), BF16),
            pltpu.VMEM((rows, width), F32),
            pltpu.VMEM((LHEADS, DH), F32),
            pltpu.VMEM((DH, LHEADS), F32),
            pltpu.VMEM((16,) + state, F32),
            pltpu.VMEM((16,) + state, BF16),
            pltpu.VMEM((16,) + state, BF16),
            pltpu.VMEM((NZ, 2) + state, BF16),
            pltpu.VMEM((NZ, 2) + state, BF16),
            pltpu.VMEM((NZ, 2) + state, BF16),
            pltpu.VMEM((NZ, 2) + state, BF16),
            pltpu.VMEM((2, 2, NZ) + state, BF16),
            pltpu.VMEM((2, NZ) + state, BF16),
            pltpu.VMEM((rows, width), F32),
            pltpu.VMEM((2,) + state, F32),
            pltpu.VMEM((2,) + state, F32),
            pltpu.VMEM((2,) + state, F32),
            pltpu.VMEM((2, LHEADS, DH), F32),
            pltpu.VMEM((NZ, 8, LHEADS), F32),
            pltpu.VMEM(state, F32),
            pltpu.VMEM((LHEADS, rows), BF16),
            dma((6,)),
            dma((2, 2, 4)), dma((2, 2, 4)),
            dma((2, 4)), dma((2, 4)),
            dma, dma((2,)),
            dma, dma,
            dma, dma,
            dma((7,)), dma((7,)),
            dma((7,)), dma((7,)),
            dma((2, 7)), dma((2, 7)),
            dma, dma,
            dma, dma((2,)),
            dma((2,)), dma((2,)),
            dma((2, 2, 4, 2)), dma((2, 2, 4, 2)),
            dma((2, 4)), dma((2, 4)),
            dma,
        ],
        compiler_params=pltpu.CompilerParams(
            collective_id=0, has_side_effects=True, vmem_limit_bytes=62 * 2**20
        ),
        name="window",
    )(
        query_lin, key_lin, value_lin, log_decay.T, out_gate, norm_gain.reshape(1, width), state_in,
        query_soft, key_soft, value_soft,
    )
    return pl.pallas_call(
        hand_over,
        out_shape=shapes,
        in_specs=[hbm, hbm, hbm],
        out_specs=(hbm, hbm, hbm),
        scratch_shapes=[
            pltpu.VMEM((rows, width), BF16),
            pltpu.VMEM(state_in.shape, F32),
            pltpu.VMEM((rows, width), BF16),
            dma((2, 9)),
        ],
        compiler_params=pltpu.CompilerParams(vmem_limit_bytes=62 * 2**20),
        name="hand_over",
    )(*results)


def solution(mesh):
    rows = P(("dp", "seq"), None)
    states = P(("dp", "seq"), None, None)
    return jax.shard_map(
        shards,
        mesh=mesh,
        in_specs=(rows, rows, rows, rows, rows, P(), states, rows, rows, rows),
        out_specs=(rows, states, rows),
        check_vma=False,
    )
```
